32 devices in a mesh: blk: 8 (over y, x, core), head: 4 (over z).
Axes of the slice: x: 2, y: 2, z: 4, core: 2. Of those that a mesh axis runs over, the one named last changes fastest.
Arguments:
- tokens: bfloat16 [3072, 1024], P(('blk', 'head')), may hold values from -18 to 18
- block_order: int32 [16], replicated, may hold values from 0 to 15, as said below
- request_lengths: int32 [9], replicated, may hold values from 1 to 2304, 3072 in all
- enc_lengths: int32 [9], replicated, may hold values from 1 to 512, 2048 in all
- w_qkv: bfloat16 [3, 1024, 1024], P(None, None, 'head'), may hold values from -0.1875 to 0.1875
- w_out: bfloat16 [1024, 1024], P('head'), may hold values from -0.1875 to 0.1875
- enc_kv: bfloat16 [2, 2048, 1024], P(None, 'blk', 'head'), may hold values from -18 to 18
- w_cq: bfloat16 [1024, 1024], replicated, may hold values from -0.1875 to 0.1875
- w_co: bfloat16 [1024, 1024], replicated, may hold values from -0.1875 to 0.1875
- w_up: bfloat16 [1024, 4096], replicated, may hold values from -0.1875 to 0.1875
- w_down: bfloat16 [4096, 1024], replicated, may hold values from -0.09375 to 0.09375
- w_next: bfloat16 [3, 1024, 1024], P(None, None, 'head'), may hold values from -0.1875 to 0.1875
Outputs:
- output: float32 [3072, 1024], P(('blk', 'head'))
- cache: bfloat16 [2, 3072, 1024], P(None, 'blk', 'head')
- next_qkv: float32 [3, 3072, 1024], P(None, 'blk', 'head')
The draws below stay inside these ranges and needn't reach their ends.
Inputs may be any that keep to these rules, and one draw needn't show every extreme that they name: `block_order`: each half-block index appears once, and stored half-blocks 2i and 2i + 1 hold position blocks that add up to 15. `request_lengths`: the lengths sum to 3072. `enc_lengths`: the lengths sum to 2048.
All inputs are finite; a program needn't handle non-finite values.
Results may differ from the reference program's by a relative error of at most 0.024.
Values may be sent and summed in bfloat16 or wider, within the bound.
No kernel may reach another device: no remote copies, remote signals or barrier semaphores. Data moves between devices by JAX's collectives and lax.ppermute only.
A program may use at most 128 MiB of HBM per device.

```python
import math
import jax
import jax.numpy as jnp
import numpy as np
from jax import lax

D = 1024
HEADS = 16
FF = 4096
HD = 64
REQS = 9
TOK_DEV = 384
ENC = 2048
TOKENS = 3072


def scaled_rows(key, shape_rows, shape_cols):
    first = jax.random.fold_in(key, 0)
    values = jnp.clip(jax.random.normal(first, (shape_rows, shape_cols), jnp.float32), -6.0, 6.0)
    return values


def draw_tokens(key, part):
    return scaled_rows(key, TOKENS, D).astype(jnp.bfloat16)


def draw_enc_kv(key, part):
    key_part = scaled_rows(jax.random.fold_in(key, 11), ENC, D)
    value_part = scaled_rows(jax.random.fold_in(key, 12), ENC, D)
    return jnp.stack([key_part, value_part]).astype(jnp.bfloat16)


def draw_block_order(key, part):
    blocks = TOKENS // TOK_DEV
    chosen = jax.random.permutation(jax.random.fold_in(key, 21), blocks).astype(jnp.int32)
    mirror = (2 * blocks - 1 - chosen).astype(jnp.int32)
    flips = jax.random.randint(jax.random.fold_in(key, 22), (blocks,), 0, 2)
    first = jnp.where(flips == 1, mirror, chosen)
    later = jnp.where(flips == 1, chosen, mirror)
    return jnp.stack([first, later], axis=1).reshape(2 * blocks).astype(jnp.int32)


def block_scale(stream_key, shape, pieces, least, top_value):
    def one(dim, shards_of):
        draws = jax.random.uniform(jax.random.fold_in(jax.random.fold_in(stream_key, 6), dim), (shards_of,), jnp.float32, least / len(pieces), top_value / len(pieces))
        return jnp.repeat(jnp.exp(draws), shape[dim] // shards_of).reshape((-1,) + (1,) * (len(shape) - dim - 1))

    gain = one(*pieces[0])
    for cut in pieces[1:]:
        gain = gain * one(*cut)
    return gain


def length_profile(count, total, most, slope):
    loads = [(1 << 20) // math.isqrt(standing ** slope) + 1 for standing in range(2, count + 1)]
    surplus, given = total - most - (count - 1), [1] * (count - 1)
    while surplus > 0:
        free = [i for i in range(count - 1) if given[i] < most]
        whole, left = sum([loads[i] for i in free]), surplus
        for i in free:
            addition = min(most - given[i], max(1, left * loads[i] // whole), surplus)
            given[i] = given[i] + addition
            surplus = surplus - addition
    return np.array([most] + given)


def uneven(rng, amount, total, reach, lean):
    if amount == 2:
        one = jax.random.randint(rng, (), max(1, total - reach), min(reach, total - 1) + 1)
        return jnp.stack([one, total - one])
    sizes = jnp.asarray(length_profile(amount, total, reach, lean), jnp.int32)
    twos = (amount - 1) // 2
    source_of, sink = sizes[1:1 + 2 * twos:2], sizes[2:2 + 2 * twos:2]
    room = jnp.minimum(source_of - 1, reach - sink)
    shifted = jax.random.randint(jax.random.fold_in(rng, 1), (twos,), 0, 1 << 20) % (room + 1)
    sizes = sizes.at[1:1 + 2 * twos:2].set(source_of - shifted).at[2:2 + 2 * twos:2].set(sink + shifted)
    return sizes[jax.random.permutation(jax.random.fold_in(rng, 2), amount)]


def bell_draw(own_key, extent, scale, limit, cuts=(), kind=jnp.bfloat16):
    gain = block_scale(own_key, extent, cuts, -0.22, 0.18) if cuts else 1.0
    array = jax.random.normal(own_key, extent, jnp.float32) * scale * gain
    return jnp.minimum(jnp.maximum(array, -limit), limit).astype(kind)


def setup_inputs(seed: int = 0) -> dict:
    keys = jax.random.split(jax.random.key(seed), 13)
    return {
        "tokens": draw_tokens(jax.random.fold_in(keys[12], 71), 0),
        "block_order": draw_block_order(jax.random.fold_in(keys[12], 71), 0),
        "request_lengths": uneven(keys[2], REQS, TOKENS, TOKENS * 3 // 4, 0).astype(jnp.int32),
        "enc_lengths": uneven(keys[3], REQS, ENC, ENC // 4, 2).astype(jnp.int32),
        "w_qkv": bell_draw(keys[4], (3, D, D), D ** -0.5, 0.1875, ((2, 4),)),
        "w_out": bell_draw(keys[5], (D, D), D ** -0.5, 0.1875, ((0, 4),)),
        "enc_kv": draw_enc_kv(jax.random.fold_in(keys[12], 71), 0),
        "w_cq": bell_draw(keys[7], (D, D), D ** -0.5, 0.1875),
        "w_co": bell_draw(keys[8], (D, D), D ** -0.5, 0.1875),
        "w_up": bell_draw(keys[9], (D, FF), D ** -0.5, 0.1875),
        "w_down": bell_draw(keys[10], (FF, D), FF ** -0.5, 0.09375),
        "w_next": bell_draw(keys[11], (3, D, D), D ** -0.5, 0.1875, ((2, 4),)),
    }


NEGATIVE = -1e+30
EPSILON = 1e-05

def normalize(matrix):
    center = matrix - lax.optimization_barrier(jnp.mean(matrix, axis=-1, keepdims=True))
    return center * lax.rsqrt(lax.optimization_barrier(jnp.mean(center * center, axis=-1, keepdims=True)) + EPSILON)

def group_of(places, lengths):
    ends = jnp.cumsum(lengths).astype(jnp.int32)
    return lax.optimization_barrier(jnp.sum((places[:, None] >= ends[None, :]).astype(jnp.int32), axis=1)).astype(jnp.int32)

def attention(queries, key_rows, value_rows, query_places, key_places, query_groups, key_groups):
    count_q = queries.shape[0]
    count_k = key_rows.shape[0]
    query_heads = queries.reshape(count_q, HEADS, HD).transpose(1, 0, 2)
    key_heads = key_rows.reshape(count_k, HEADS, HD).transpose(1, 0, 2)
    value_heads = value_rows.reshape(count_k, HEADS, HD).transpose(1, 0, 2)
    place_blocks = query_places.reshape(-1, TOK_DEV)
    group_blocks = query_groups.reshape(-1, TOK_DEV)

    def per_head(element):
        query_one, key_one, value_one = element
        query_blocks = query_one.reshape(-1, TOK_DEV, HD)

        def per_block(paired):
            query_block, place_block, group_block = paired
            scores = jnp.dot(query_block, key_one.T, preferred_element_type=jnp.float32) * 0.125
            visible = key_groups[None, :] == group_block[:, None]
            if key_places is not None:
                visible = visible & (key_places[None, :] <= place_block[:, None])
            scores = jnp.where(visible, scores, NEGATIVE)
            maxima = lax.optimization_barrier(jnp.max(scores, axis=1, keepdims=True))
            weights = jnp.where(visible, jnp.exp(scores - maxima), 0.0)
            totals = lax.optimization_barrier(jnp.sum(weights, axis=1, keepdims=True))
            return jnp.dot(weights.astype(jnp.bfloat16), value_one, preferred_element_type=jnp.float32) / totals
        return lax.map(per_block, (query_blocks, place_blocks, group_blocks)).reshape(count_q, HD)
    merged = lax.map(per_head, (query_heads, key_heads, value_heads))
    return merged.transpose(1, 0, 2).reshape(count_q, D).astype(jnp.bfloat16)

def reference(tokens, block_order, request_lengths, enc_lengths, w_qkv, w_out, enc_kv, w_cq, w_co, w_up, w_down, w_next):
    halfway = TOK_DEV // 2
    indices = jnp.arange(TOKENS, dtype=jnp.int32)
    position = (block_order[indices // halfway] * halfway + indices % halfway).astype(jnp.int32)
    request = group_of(position, request_lengths)
    enc_request = group_of(jnp.arange(ENC, dtype=jnp.int32), enc_lengths)
    query = jnp.dot(tokens, w_qkv[0], preferred_element_type=jnp.float32).astype(jnp.bfloat16)
    key_all = jnp.dot(tokens, w_qkv[1], preferred_element_type=jnp.float32).astype(jnp.bfloat16)
    value_all = jnp.dot(tokens, w_qkv[2], preferred_element_type=jnp.float32).astype(jnp.bfloat16)
    stored_kv = jnp.stack([key_all, value_all])
    cache = jnp.zeros_like(stored_kv).at[:, position].set(stored_kv)
    attended = attention(query, key_all, value_all, position, position, request, request)
    hidden = normalize(jnp.dot(attended, w_out, preferred_element_type=jnp.float32) + tokens.astype(jnp.float32))
    hidden_b = hidden.astype(jnp.bfloat16)
    cross_query = jnp.dot(hidden_b, w_cq, preferred_element_type=jnp.float32).astype(jnp.bfloat16)
    crossed = attention(cross_query, enc_kv[0], enc_kv[1], position, None, request, enc_request)
    second = normalize(jnp.dot(crossed, w_co, preferred_element_type=jnp.float32) + hidden)
    second_b = second.astype(jnp.bfloat16)
    inner = jax.nn.gelu(jnp.dot(second_b, w_up, preferred_element_type=jnp.float32), approximate=False).astype(jnp.bfloat16)
    output = normalize(jnp.dot(inner, w_down, preferred_element_type=jnp.float32) + second)
    output_b = output.astype(jnp.bfloat16)
    next_qkv = jnp.stack([jnp.dot(output_b, w_next[0], preferred_element_type=jnp.float32), jnp.dot(output_b, w_next[1], preferred_element_type=jnp.float32), jnp.dot(output_b, w_next[2], preferred_element_type=jnp.float32)])
    return (output, cache, next_qkv)
```

```python
import functools

import jax
import jax.numpy as jnp
from jax import lax
from jax.experimental import pallas as pl
from jax.experimental.pallas import tpu as pltpu
from jax.sharding import PartitionSpec as P

HEADS = 16
NEGATIVE = -1e30
SCALING = 0.125
EPSILON = 1e-05
TILE = 256
MIB = 1024 * 1024


def whole(count):
    return [pl.BlockSpec(memory_space=pltpu.VMEM)] * count


def smem(count):
    return [pl.BlockSpec(memory_space=pltpu.SMEM)] * count


def params(mib):
    return pltpu.CompilerParams(vmem_limit_bytes=mib * MIB)


def xor(size, bits):
    return [(i, i ^ bits) for i in range(size)]


def normalize(matrix):
    center = matrix - jnp.mean(matrix, axis=-1, keepdims=True)
    return center * lax.rsqrt(jnp.mean(center * center, axis=-1, keepdims=True) + EPSILON)


def project_kernel(spots_ref, x0, x1, w_ref, x_ref, q_ref, kv_ref):
    quarter = x0.shape[0]
    for i, piece in enumerate((x0, x1)):
        x_ref[pl.ds(pl.multiple_of(spots_ref[i] % 2 * quarter, quarter), quarter), :] = piece[...]
    x = x_ref[...]
    q_ref[...] = jnp.dot(x, w_ref[0], preferred_element_type=jnp.float32).astype(jnp.bfloat16)
    for c in range(2):
        kv_ref[c] = jnp.dot(x, w_ref[1 + c], preferred_element_type=jnp.float32).astype(
            jnp.bfloat16
        )


def project(spots, x0, x1, w_qkv):
    rows, width, model = 2 * x0.shape[0], w_qkv.shape[2], x0.shape[1]
    return pl.pallas_call(
        project_kernel,
        out_shape=(
            jax.ShapeDtypeStruct((rows, model), jnp.bfloat16),
            jax.ShapeDtypeStruct((rows, width), jnp.bfloat16),
            jax.ShapeDtypeStruct((2, rows, width), jnp.bfloat16),
        ),
        in_specs=smem(1) + whole(3),
        out_specs=tuple(whole(3)),
        compiler_params=params(8),
        name="project",
    )(spots, x0, x1, w_qkv)


def place_kernel(count, dest_ref, *refs):
    out_ref = refs[count]
    for i in range(count):
        rows = refs[i].shape[0]
        out_ref[pl.ds(pl.multiple_of(dest_ref[i] * rows, rows), rows), :] = refs[i][...]


def place(chunks, dest):
    count = len(chunks)
    rows, columns = chunks[0].shape
    return pl.pallas_call(
        functools.partial(place_kernel, count),
        out_shape=jax.ShapeDtypeStruct((rows * count, columns), chunks[0].dtype),
        in_specs=smem(1) + whole(count),
        out_specs=whole(1)[0],
        compiler_params=params(8),
        name="place",
    )(dest, *chunks)


def order_kernel(count, cached, dest_ref, *refs):
    k_ref, v_ref = refs[count], refs[count + 1]
    held_ref, sem = refs[-2], refs[-1]
    copies, index = [], 0
    for i in range(count):
        pieces, rows = refs[i].shape[0], refs[i].shape[2]
        for piece in range(pieces):
            at = pl.ds(pl.multiple_of(dest_ref[index] * rows, rows), rows)
            for c, to in enumerate((k_ref, held_ref)):
                copy = pltpu.make_async_copy(refs[i].at[piece, c], to.at[at, :], sem)
                copy.start()
                copies.append(copy)
            index += 1
    for copy in copies:
        copy.wait()
    lane = lax.broadcasted_iota(jnp.int32, (TILE, 128), 1) // 64

    def step(tile, carry):
        at = pl.ds(pl.multiple_of(tile * TILE, TILE), TILE)
        for head in range(v_ref.shape[0]):
            pair = held_ref[at, (head // 2) * 128 : (head // 2 + 1) * 128]
            v_ref[head, at, :] = jnp.where(lane == head % 2, pair, jnp.ones_like(pair))
        return carry

    lax.fori_loop(0, held_ref.shape[0] // TILE, step, 0)
    if cached:
        cache_ref = refs[count + 2]
        length = cache_ref.shape[1]
        at = pl.ds(pl.multiple_of(dest_ref[index] * length, length), length)
        cache_ref[0] = k_ref[at, :]
        cache_ref[1] = held_ref[at, :]


def order(chunks, dest, cached):
    rows, width = chunks[0].shape[2:]
    total = rows * sum(c.shape[0] for c in chunks)
    heads = width // 64
    outs = [
        jax.ShapeDtypeStruct((total, width), jnp.bfloat16),
        jax.ShapeDtypeStruct((heads, total, 128), jnp.bfloat16),
    ]
    if cached:
        outs.append(jax.ShapeDtypeStruct((2, cached, width), jnp.bfloat16))
    return pl.pallas_call(
        functools.partial(order_kernel, len(chunks), bool(cached)),
        out_shape=tuple(outs),
        in_specs=smem(1) + [pl.BlockSpec(memory_space=pltpu.HBM)] * len(chunks),
        out_specs=tuple(whole(len(outs))),
        scratch_shapes=[pltpu.VMEM((total, width), jnp.bfloat16), pltpu.SemaphoreType.DMA],
        compiler_params=params(4 + 2 * total * width * 2 // MIB),
        name="order",
    )(dest, *chunks)


def flash(queries, k_ref, v_ref, low, high, first, last):
    rows, width = queries.shape
    heads = width // 64
    lane = lax.broadcasted_iota(jnp.int32, (rows, 128), 1) // 64
    masked = []
    for head in range(heads):
        pair = queries[:, (head // 2) * 128 : (head // 2 + 1) * 128]
        pair = (pair.astype(jnp.float32) * SCALING).astype(jnp.bfloat16)
        masked.append(jnp.where(lane == head % 2, pair, jnp.zeros_like(pair)))

    def step(tile, carry):
        start = pl.multiple_of(tile * TILE, TILE)
        keys = start + lax.broadcasted_iota(jnp.int32, (rows, TILE), 1)
        seen = (keys >= low) & (keys < high)
        bias = jnp.where(seen, 0.0, NEGATIVE)
        after = []
        for head in range(heads):
            peak, total = carry[head]
            at = slice((head // 2) * 128, (head // 2 + 1) * 128)
            scores = lax.dot_general(
                masked[head],
                k_ref[pl.ds(start, TILE), at],
                (((1,), (1,)), ((), ())),
                preferred_element_type=jnp.float32,
            )
            scores = scores + bias
            top = jnp.maximum(peak, jnp.max(scores, axis=1, keepdims=True))
            weights = jnp.exp(scores - top)
            total = total * jnp.exp(peak - top) + jnp.dot(
                weights.astype(jnp.bfloat16),
                v_ref[head, pl.ds(start, TILE), :],
                preferred_element_type=jnp.float32,
            )
            after.append((top, total))
        return tuple(after)

    begin = tuple(
        (jnp.full((rows, 1), NEGATIVE, jnp.float32), jnp.zeros((rows, 128), jnp.float32))
        for _ in range(heads)
    )
    carry = lax.fori_loop(first, last + 1, step, begin)
    outs = []
    for pair in range(heads // 2):
        even, odd = carry[2 * pair][1], carry[2 * pair + 1][1]
        sums = pltpu.roll(jnp.where(lane == 0, odd, even), 64, 1)
        outs.append(jnp.where(lane == 0, even, odd) / sums)
    return jnp.concatenate(outs, axis=1)


def self_kernel(half, order_ref, ends_ref, spots_ref, near_ref, far_ref, k_ref, v_ref, out_ref):
    rows = near_ref.shape[0]
    queries = jnp.where(spots_ref[0] // 2 == half, near_ref[...], far_ref[...])
    base = order_ref[half] * rows
    places = base + lax.broadcasted_iota(jnp.int32, (rows, 1), 0)
    low = jnp.zeros((rows, 1), jnp.int32)
    least = jnp.int32(0)
    for j in range(ends_ref.shape[0]):
        end = ends_ref[j]
        low = jnp.where(places >= end, end, low)
        least = jnp.where(base >= end, end, least)
    result = flash(
        queries,
        k_ref,
        v_ref,
        low,
        places + 1,
        least // TILE,
        (base + rows - 1) // TILE,
    )
    out_ref[...] = result.astype(jnp.bfloat16)


def self_attention(half, pair, ends, spots, near, far, keys, values):
    return pl.pallas_call(
        functools.partial(self_kernel, half),
        out_shape=jax.ShapeDtypeStruct(near.shape, jnp.bfloat16),
        in_specs=smem(3) + whole(4),
        out_specs=whole(1)[0],
        compiler_params=params(8),
        name="self_attention",
    )(pair, ends, spots, near, far, keys, values)


def cross_kernel(
    half, order_ref, ends_ref, encs_ref, spots_ref,
    a0, a1, a2, a3, near_ref, far_ref, wo_ref, wq_ref, k_ref, v_ref, hidden_ref, out_ref,
):
    rows, width = a0.shape
    mixed = jnp.where(spots_ref[0] // 2 == half, near_ref[...], far_ref[...]).astype(jnp.float32)
    for i, piece in enumerate((a0, a1, a2, a3)):
        at = pl.ds(pl.multiple_of(spots_ref[i] * width, width), width)
        mixed = mixed + jnp.dot(piece[...], wo_ref[at, :], preferred_element_type=jnp.float32)
    hidden = normalize(mixed)
    hidden_ref[...] = hidden
    queries = jnp.dot(
        hidden.astype(jnp.bfloat16), wq_ref[...], preferred_element_type=jnp.float32
    ).astype(jnp.bfloat16)
    base = order_ref[half] * rows
    places = base + lax.broadcasted_iota(jnp.int32, (rows, 1), 0)
    count = ends_ref.shape[0]
    low = jnp.zeros((rows, 1), jnp.int32)
    least = jnp.int32(0)
    for j in range(count):
        low = jnp.where(places >= ends_ref[j], encs_ref[j], low)
        least = jnp.where(base >= ends_ref[j], encs_ref[j], least)
    high = jnp.full((rows, 1), encs_ref[count - 1], jnp.int32)
    most = encs_ref[count - 1]
    for j in reversed(range(count)):
        high = jnp.where(places < ends_ref[j], encs_ref[j], high)
        most = jnp.where(base + rows - 1 < ends_ref[j], encs_ref[j], most)
    result = flash(queries, k_ref, v_ref, low, high, least // TILE, (most - 1) // TILE)
    out_ref[...] = result.astype(jnp.bfloat16)


def cross_attention(
    half, pair, ends, encs, spots, pieces, near, far, w_out, w_cq, keys, values
):
    rows, width = pieces[0].shape
    return pl.pallas_call(
        functools.partial(cross_kernel, half),
        out_shape=(
            jax.ShapeDtypeStruct(near.shape, jnp.float32),
            jax.ShapeDtypeStruct((rows, width), jnp.bfloat16),
        ),
        in_specs=smem(4) + whole(10),
        out_specs=tuple(whole(2)),
        compiler_params=params(12),
        name="cross_attention",
    )(pair, ends, encs, spots, *pieces, near, far, w_out, w_cq, keys, values)


def fetch_kernel(count, *refs):
    sem = refs[-1]
    copies = []
    for i in range(count):
        copy = pltpu.make_async_copy(refs[i], refs[count + i], sem)
        copy.start()
        copies.append(copy)
    for copy in copies:
        copy.wait()


def fetch(arrays):
    return pl.pallas_call(
        functools.partial(fetch_kernel, len(arrays)),
        out_shape=tuple(jax.ShapeDtypeStruct(a.shape, a.dtype) for a in arrays),
        in_specs=[pl.BlockSpec(memory_space=pltpu.HBM)] * len(arrays),
        out_specs=tuple(whole(len(arrays))),
        scratch_shapes=[pltpu.SemaphoreType.DMA],
        compiler_params=params(1),
        name="fetch",
    )(*arrays)


def mlp_kernel(
    spots_ref, c0, c1, c2, c3, hidden_ref, wco_ref, up_ref, down_ref, wn_ref,
    out_ref, next_ref, bf_ref, sum_ref,
):
    width = c0.shape[1]
    mixed = hidden_ref[...]
    for i, piece in enumerate((c0, c1, c2, c3)):
        at = pl.ds(pl.multiple_of(spots_ref[i] * width, width), width)
        mixed = mixed + jnp.dot(piece[...], wco_ref[at, :], preferred_element_type=jnp.float32)
    second = normalize(mixed)
    bf_ref[...] = second.astype(jnp.bfloat16)
    sum_ref[...] = second
    part = 1024

    def step(i, carry):
        at = pl.ds(pl.multiple_of(i * part, part), part)
        raised = jnp.dot(bf_ref[...], up_ref[:, at], preferred_element_type=jnp.float32)
        inner = (raised * (1.0 + lax.erf(raised * (0.5**0.5))) * 0.5).astype(jnp.bfloat16)
        sum_ref[...] += jnp.dot(inner, down_ref[at, :], preferred_element_type=jnp.float32)
        return carry

    lax.fori_loop(0, up_ref.shape[1] // part, step, 0)
    output = normalize(sum_ref[...])
    out_ref[...] = output
    output_b = output.astype(jnp.bfloat16)
    for c in range(3):
        next_ref[c] = jnp.dot(output_b, wn_ref[c], preferred_element_type=jnp.float32)


def mlp(spots, pieces, hidden, w_co, w_up, w_down, w_next):
    rows, width = pieces[0].shape
    model = w_up.shape[0]
    return pl.pallas_call(
        mlp_kernel,
        out_shape=(
            jax.ShapeDtypeStruct((rows, model), jnp.float32),
            jax.ShapeDtypeStruct((3, rows, width), jnp.float32),
        ),
        in_specs=smem(1) + whole(9),
        out_specs=tuple(whole(2)),
        scratch_shapes=[
            pltpu.VMEM((rows, model), jnp.bfloat16),
            pltpu.VMEM((rows, model), jnp.float32),
        ],
        compiler_params=params(12),
        name="mlp",
    )(spots, *pieces, hidden, w_co, w_up, w_down, w_next)


def over_head(x, size):
    return [x] + [lax.ppermute(x, "head", xor(size, j)) for j in range(1, size)]


def over_plane(x, size):
    me = lax.axis_index("blk")
    if size != 8:
        return [lax.all_gather(x, "blk", axis=0)], [jnp.int32(s) for s in range(size)]
    near = [(s, x if s == 0 else lax.ppermute(x, "blk", xor(size, s))) for s in (0, 2, 4, 6)]
    far = [(s + 1, lax.ppermute(y, "blk", xor(size, 1))) for s, y in near]
    return [y[None] for _, y in near + far], [me ^ s for s, _ in near + far]


def on_device(
    tokens, block_order, request_lengths, enc_lengths, w_qkv, w_out, enc_kv, w_cq, w_co, w_up,
    w_down, w_next,
):
    quarter = tokens.shape[0]
    group = lax.axis_size("head")
    cycle = lax.axis_size("blk")
    me = lax.axis_index("blk")
    member = lax.axis_index("head")
    width = w_qkv.shape[2]
    ends = jnp.cumsum(request_lengths).astype(jnp.int32)
    encs = jnp.cumsum(enc_lengths).astype(jnp.int32)
    pair = lax.dynamic_slice_in_dim(block_order, 2 * me, 2, 0)
    spots = member ^ jnp.arange(group, dtype=jnp.int32)

    rows = over_head(tokens, group)
    w_co, w_up, w_down, w_next = fetch((w_co, w_up, w_down, w_next))
    queries, xs, shards, dest = [], [], [], []
    for far in range(2):
        x, q, kv = project(spots[2 * far : 2 * far + 2], rows[2 * far], rows[2 * far + 1], w_qkv)
        queries.append(q)
        xs.append(x)
        arrays, sources = over_plane(kv, cycle)
        shards += arrays
        dest += [block_order[2 * source + (member // 2 ^ far)] for source in sources]
    dest.append(me)
    keys, values, cache = order(shards, jnp.stack(dest), 4 * quarter)

    enc_shards, enc_dest = over_plane(enc_kv, cycle)
    enc_keys, enc_values = order(enc_shards, jnp.stack(enc_dest), 0)
    out_rows = place(over_head(w_out, group), spots)
    cq_columns = lax.dynamic_slice_in_dim(w_cq, member * width, width, 1)

    outs, nexts = [], []
    for half in range(2):
        attended = self_attention(half, pair, ends, spots, *queries, keys, values)
        hidden, crossed = cross_attention(
            half, pair, ends, encs, spots, over_head(attended, group), *xs, out_rows, cq_columns,
            enc_keys, enc_values,
        )
        output, next_half = mlp(
            spots, over_head(crossed, group), hidden, w_co, w_up, w_down, w_next
        )
        outs.append(output)
        nexts.append(next_half)
    output = lax.dynamic_slice_in_dim(
        jnp.concatenate(outs, axis=0), member * quarter, quarter, 0
    )
    return (output, cache, jnp.concatenate(nexts, axis=1))


def solution(mesh):
    in_specs = (
        P(("blk", "head"), None),
        P(),
        P(),
        P(),
        P(None, None, "head"),
        P("head", None),
        P(None, "blk", "head"),
        P(),
        P(),
        P(),
        P(),
        P(None, None, "head"),
    )
    out_specs = (P(("blk", "head"), None), P(None, "blk", "head"), P(None, "blk", "head"))
    return jax.shard_map(
        on_device, mesh=mesh, in_specs=in_specs, out_specs=out_specs, check_vma=False
    )
```

```python
import functools
import math

import jax
import jax.numpy as jnp
from jax import lax
from jax.experimental import pallas as pl
from jax.experimental.pallas import tpu as pltpu
from jax.sharding import PartitionSpec as P

HEADS = 16
NEGATIVE = -1e30
SCALING = 0.125
EPSILON = 1e-05
TILE = 256
MIB = 1024 * 1024


def whole(count):
    return [pl.BlockSpec(memory_space=pltpu.VMEM)] * count


def anywhere(count):
    return [pl.BlockSpec(memory_space=pl.ANY)] * count


def smem(count):
    return [pl.BlockSpec(memory_space=pltpu.SMEM)] * count


def params(mib):
    return pltpu.CompilerParams(vmem_limit_bytes=mib * MIB)


def xor(size, bits):
    return [(i, i ^ bits) for i in range(size)]


def normalize(matrix):
    center = matrix - jnp.mean(matrix, axis=-1, keepdims=True)
    return center * lax.rsqrt(jnp.mean(center * center, axis=-1, keepdims=True) + EPSILON)


def cost(flops, moved):
    return pl.CostEstimate(flops=int(flops) // 20, bytes_accessed=int(moved) // 20, transcendentals=0)


def skipping(kernel, at, count):
    def body(*refs):
        kernel(*refs[:at], *refs[at + count :])

    return body


def rows_at(index, rows):
    return pl.ds(pl.multiple_of(index * rows, rows), rows)


def sums_of(lengths_ref):
    sums, total = [], jnp.int32(0)
    for j in range(lengths_ref.shape[0]):
        total = total + lengths_ref[j]
        sums.append(total)
    return sums


def project_kernel(ids_ref, x0, x1, x2, x3, w_ref, wo_ref, x_ref, q_ref, kv_ref, part_ref):
    part_ref[...] = wo_ref[rows_at(ids_ref[0] % 2, part_ref.shape[0]), :]
    for i, piece in enumerate((x0, x1, x2, x3)):
        x_ref[rows_at(ids_ref[1] ^ i, x0.shape[0]), :] = piece[...]
    x = x_ref[...]
    for c in range(2):
        kv_ref[c] = jnp.dot(x, w_ref[1 + c], preferred_element_type=jnp.float32).astype(
            jnp.bfloat16
        )
    q_ref[...] = jnp.dot(x, w_ref[0], preferred_element_type=jnp.float32).astype(jnp.bfloat16)


def project(ids, pieces, w_qkv, w_out):
    rows, width, model = 4 * pieces[0].shape[0], w_qkv.shape[2], pieces[0].shape[1]
    return pl.pallas_call(
        project_kernel,
        out_shape=(
            jax.ShapeDtypeStruct((rows, model), jnp.bfloat16),
            jax.ShapeDtypeStruct((rows, width), jnp.bfloat16),
            jax.ShapeDtypeStruct((2, rows, width), jnp.bfloat16),
            jax.ShapeDtypeStruct((width // 2, w_out.shape[1]), jnp.bfloat16),
        ),
        in_specs=smem(1) + whole(6),
        out_specs=tuple(whole(4)),
        compiler_params=params(4),
        cost_estimate=cost(2 * rows * model * 3 * width, 2 * 3 * model * width),
        name="project",
    )(ids, *pieces, w_qkv, w_out)


def fetch_kernel(count, columns, ids_ref, *refs):
    sem = refs[-1]
    copies = []
    for i in range(count):
        source, target = refs[i], refs[count + i]
        if i in columns:
            width = target.shape[1]
            source = source.at[:, pl.ds(pl.multiple_of(ids_ref[1] * width, width), width)]
        copy = pltpu.make_async_copy(source, target, sem)
        copy.start()
        copies.append(copy)
    for copy in copies:
        copy.wait()


def fetch(ids, arrays, columns, room, after):
    count = len(arrays)
    shapes = [(a.shape[0], columns[i]) if i in columns else a.shape for i, a in enumerate(arrays)]
    return pl.pallas_call(
        skipping(functools.partial(fetch_kernel, count, columns), 1 + count, len(after)),
        out_shape=tuple(jax.ShapeDtypeStruct(s, a.dtype) for s, a in zip(shapes, arrays)),
        in_specs=smem(1) + anywhere(count + len(after)),
        out_specs=tuple(whole(count)),
        scratch_shapes=[pltpu.SemaphoreType.DMA],
        compiler_params=params(room),
        cost_estimate=cost(0, 2 * sum(math.prod(s) for s in shapes)),
        name="fetch",
    )(ids, *arrays, *after)


def bundle_kernel(groups, *refs):
    at = sum(groups)
    for i, count in enumerate(groups):
        for j in range(count):
            refs[at + i][j] = refs[sum(groups[:i]) + j][...]


def bundle(groups, after):
    counts = [len(g) for g in groups]
    total = sum(counts)
    return pl.pallas_call(
        skipping(functools.partial(bundle_kernel, counts), total, len(after)),
        out_shape=tuple(jax.ShapeDtypeStruct((len(g),) + g[0].shape, g[0].dtype) for g in groups),
        in_specs=whole(total) + anywhere(len(after)),
        out_specs=tuple(whole(len(groups))),
        compiler_params=params(2),
        cost_estimate=cost(0, 2 * 2 * sum(len(g) * math.prod(g[0].shape) for g in groups)),
        name="bundle",
    )(*[x for g in groups for x in g], *after)


def spread(values, v_ref, at):
    lane = lax.broadcasted_iota(jnp.int32, (values.shape[0], 128), 1) // 64
    for head in range(v_ref.shape[0]):
        pair = values[:, (head // 2) * 128 : (head // 2 + 1) * 128]
        v_ref[head, at, :] = jnp.where(lane == head % 2, pair, jnp.ones_like(pair))


def order_kernel(sources, ids_ref, order_ref, *refs):
    k_ref, v_ref, cache_ref = refs[-3:]
    for ref, (relative, numbers) in zip(refs, sources):
        rows = ref.shape[2] // 2
        for piece, number in enumerate(numbers):
            block = ids_ref[0] ^ number if relative else jnp.int32(number)
            for half in range(2):
                at = rows_at(order_ref[2 * block + half], rows)
                here = slice(half * rows, (half + 1) * rows)
                k_ref[at, :] = ref[piece, 0, here, :]
                spread(ref[piece, 1, here, :], v_ref, at)
    length = cache_ref.shape[1]
    at = rows_at(ids_ref[0], length)
    cache_ref[0] = k_ref[at, :]
    lane = lax.broadcasted_iota(jnp.int32, (length, 128), 1) // 64
    for pair in range(v_ref.shape[0] // 2):
        cache_ref[1, :, pair * 128 : (pair + 1) * 128] = jnp.where(
            lane == 0, v_ref[2 * pair, at, :], v_ref[2 * pair + 1, at, :]
        )


def order(ids, block_order, chunks, sources):
    rows, width = chunks[0].shape[2:]
    total = rows * sum(c.shape[0] for c in chunks)
    return pl.pallas_call(
        functools.partial(order_kernel, sources),
        out_shape=(
            jax.ShapeDtypeStruct((total, width), jnp.bfloat16),
            jax.ShapeDtypeStruct((width // 64, total, 128), jnp.bfloat16),
            jax.ShapeDtypeStruct((2, rows, width), jnp.bfloat16),
        ),
        in_specs=smem(2) + whole(len(chunks)),
        out_specs=tuple(whole(3)),
        compiler_params=params(4),
        cost_estimate=cost(0, 5 * 2 * total * width),
        name="order",
    )(ids, block_order, *chunks)


def prepare_kernel(sources, ids_ref, *refs):
    k_ref, v_ref, w_ref = refs[-3:]
    for ref, (relative, numbers) in zip(refs, sources):
        rows = ref.shape[2]
        for piece, number in enumerate(numbers):
            at = rows_at(ids_ref[0] ^ number if relative else jnp.int32(number), rows)
            k_ref[at, :] = ref[piece, 0]
            spread(ref[piece, 1], v_ref, at)
    parts = refs[len(sources) : -3]
    for i, part in enumerate(parts):
        for j in range(part.shape[0]):
            w_ref[ids_ref[1] ^ j, ids_ref[0] % 2 ^ i] = part[j]


def prepare(ids, chunks, sources, parts):
    rows, width = chunks[0].shape[2:]
    total = rows * sum(c.shape[0] for c in chunks)
    group, depth, model = parts[0].shape
    return pl.pallas_call(
        functools.partial(prepare_kernel, sources),
        out_shape=(
            jax.ShapeDtypeStruct((total, width), jnp.bfloat16),
            jax.ShapeDtypeStruct((width // 64, total, 128), jnp.bfloat16),
            jax.ShapeDtypeStruct((group, 2, depth, model), jnp.bfloat16),
        ),
        in_specs=smem(1) + whole(len(chunks) + len(parts)),
        out_specs=tuple(whole(3)),
        compiler_params=params(4),
        cost_estimate=cost(0, 5 * 2 * total * width),
        name="prepare",
    )(ids, *chunks, *parts)


def flash(queries, k_ref, v_ref, low, high, first, last):
    rows, width = queries.shape
    heads = width // 64
    lane = lax.broadcasted_iota(jnp.int32, (rows, 128), 1) // 64
    masked = []
    for head in range(heads):
        pair = queries[:, (head // 2) * 128 : (head // 2 + 1) * 128]
        pair = (pair.astype(jnp.float32) * SCALING).astype(jnp.bfloat16)
        masked.append(jnp.where(lane == head % 2, pair, jnp.zeros_like(pair)))

    def step(tile, carry):
        start = pl.multiple_of(tile * TILE, TILE)
        keys = start + lax.broadcasted_iota(jnp.int32, (rows, TILE), 1)
        seen = (keys >= low) & (keys < high)
        bias = jnp.where(seen, 0.0, NEGATIVE)
        after = []
        for head in range(heads):
            peak, total = carry[head]
            at = slice((head // 2) * 128, (head // 2 + 1) * 128)
            scores = lax.dot_general(
                masked[head],
                k_ref[pl.ds(start, TILE), at],
                (((1,), (1,)), ((), ())),
                preferred_element_type=jnp.float32,
            )
            scores = scores + bias
            top = jnp.maximum(peak, jnp.max(scores, axis=1, keepdims=True))
            weights = jnp.exp(scores - top)
            total = total * jnp.exp(peak - top) + jnp.dot(
                weights.astype(jnp.bfloat16),
                v_ref[head, pl.ds(start, TILE), :],
                preferred_element_type=jnp.float32,
            )
            after.append((top, total))
        return tuple(after)

    begin = tuple(
        (jnp.full((rows, 1), NEGATIVE, jnp.float32), jnp.zeros((rows, 128), jnp.float32))
        for _ in range(heads)
    )
    carry = lax.fori_loop(first, last + 1, step, begin)
    outs = []
    for pair in range(heads // 2):
        even, odd = carry[2 * pair][1], carry[2 * pair + 1][1]
        sums = pltpu.roll(jnp.where(lane == 0, odd, even), 64, 1)
        outs.append(jnp.where(lane == 0, even, odd) / sums)
    return jnp.concatenate(outs, axis=1)


def half_of(turn, ids_ref, order_ref):
    first = order_ref[2 * ids_ref[0]]
    second = order_ref[2 * ids_ref[0] + 1]
    return jnp.where(first < second, turn, 1 - turn)


def self_kernel(turn, ids_ref, order_ref, lengths_ref, q_ref, k_ref, v_ref, out_ref):
    rows = out_ref.shape[0]
    half = half_of(turn, ids_ref, order_ref)
    queries = q_ref[rows_at(half, rows), :]
    base = order_ref[2 * ids_ref[0] + half] * rows
    places = base + lax.broadcasted_iota(jnp.int32, (rows, 1), 0)
    low = jnp.zeros((rows, 1), jnp.int32)
    least = jnp.int32(0)
    for end in sums_of(lengths_ref):
        low = jnp.where(places >= end, end, low)
        least = jnp.where(base >= end, end, least)
    first, last = least // TILE, (base + rows - 1) // TILE
    result = flash(queries, k_ref, v_ref, low, places + 1, first, last)
    out_ref[...] = result.astype(jnp.bfloat16)


def self_attention(turn, ids, block_order, lengths, queries, keys, values):
    rows, width = queries.shape
    return pl.pallas_call(
        functools.partial(self_kernel, turn),
        out_shape=jax.ShapeDtypeStruct((rows // 2, width), jnp.bfloat16),
        in_specs=smem(3) + whole(3),
        out_specs=whole(1)[0],
        compiler_params=params(4),
        cost_estimate=cost(5e9, 0),
        name="self_attention",
    )(ids, block_order, lengths, queries, keys, values)


def cross_kernel(
    turn, ids_ref, order_ref, lengths_ref, encs_ref,
    a0, a1, a2, a3, x_ref, wo_ref, wq_ref, k_ref, v_ref, hidden_ref, out_ref,
):
    rows, width = a0.shape
    member = ids_ref[1]
    half = half_of(turn, ids_ref, order_ref)
    mixed = x_ref[rows_at(half, rows), :].astype(jnp.float32)
    for i, piece in enumerate((a0, a1, a2, a3)):
        mixed = mixed + jnp.dot(
            piece[...], wo_ref[member ^ i], preferred_element_type=jnp.float32
        )
    hidden = normalize(mixed)
    hidden_ref[...] = hidden
    queries = jnp.dot(
        hidden.astype(jnp.bfloat16), wq_ref[...], preferred_element_type=jnp.float32
    ).astype(jnp.bfloat16)
    base = order_ref[2 * ids_ref[0] + half] * rows
    places = base + lax.broadcasted_iota(jnp.int32, (rows, 1), 0)
    ends, encs = sums_of(lengths_ref), sums_of(encs_ref)
    low = jnp.zeros((rows, 1), jnp.int32)
    least = jnp.int32(0)
    for end, enc in zip(ends, encs):
        low = jnp.where(places >= end, enc, low)
        least = jnp.where(base >= end, enc, least)
    high = jnp.full((rows, 1), encs[-1], jnp.int32)
    most = encs[-1]
    for end, enc in zip(reversed(ends), reversed(encs)):
        high = jnp.where(places < end, enc, high)
        most = jnp.where(base + rows - 1 < end, enc, most)
    result = flash(queries, k_ref, v_ref, low, high, least // TILE, (most - 1) // TILE)
    out_ref[...] = result.astype(jnp.bfloat16)


def cross_attention(turn, ids, block_order, lengths, encs, pieces, x, w_out, w_cq, keys, values):
    rows, width = pieces[0].shape
    model = x.shape[1]
    return pl.pallas_call(
        functools.partial(cross_kernel, turn),
        out_shape=(
            jax.ShapeDtypeStruct((rows, model), jnp.float32),
            jax.ShapeDtypeStruct((rows, width), jnp.bfloat16),
        ),
        in_specs=smem(4) + whole(9),
        out_specs=tuple(whole(2)),
        compiler_params=params(5),
        cost_estimate=cost(5e9, 0),
        name="cross_attention",
    )(ids, block_order, lengths, encs, *pieces, x, w_out, w_cq, keys, values)


PART = 1024


def mlp_kernel(
    turn, ids_ref, order_ref, c0, c1, c2, c3, hidden_ref, wco_ref, up_ref, down_ref, wn_ref, *refs
):
    out_ref, next_ref, bf_ref, sum_ref, held_ref, sems = refs[-6:]
    member = ids_ref[1]
    half = half_of(turn, ids_ref, order_ref)
    rows, width = c0.shape
    mixed = hidden_ref[...]
    for i, piece in enumerate((c0, c1, c2, c3)):
        mixed = mixed + jnp.dot(
            piece[...], wco_ref[rows_at(member ^ i, width), :], preferred_element_type=jnp.float32
        )
    second = normalize(mixed)
    bf_ref[...] = second.astype(jnp.bfloat16)
    sum_ref[...] = second
    for i in range(up_ref.shape[1] // PART):
        at = slice(i * PART, (i + 1) * PART)
        raised = jnp.dot(bf_ref[...], up_ref[:, at], preferred_element_type=jnp.float32)
        inner = (raised * (1.0 + lax.erf(raised * (0.5**0.5))) * 0.5).astype(jnp.bfloat16)
        sum_ref[...] += jnp.dot(inner, down_ref[at, :], preferred_element_type=jnp.float32)
    output = normalize(sum_ref[...])
    sum_ref[...] = output
    own = pltpu.make_async_copy(
        sum_ref.at[rows_at(member % 2, rows // 2), :], out_ref, sems.at[3]
    )

    @pl.when(member // 2 == half)
    def _():
        own.start()

    bf_ref[...] = output.astype(jnp.bfloat16)
    copies = []
    for c in range(3):
        held_ref[c] = jnp.dot(bf_ref[...], wn_ref[c], preferred_element_type=jnp.float32)
        copy = pltpu.make_async_copy(
            held_ref.at[c], next_ref.at[c, rows_at(half, rows), :], sems.at[c]
        )
        copy.start()
        copies.append(copy)
    for copy in copies:
        copy.wait()

    @pl.when(member // 2 == half)
    def _():
        own.wait()


def mlp(turn, ids, block_order, pieces, hidden, w_co, weights, before):
    rows, width = pieces[0].shape
    model = w_co.shape[0]
    return pl.pallas_call(
        functools.partial(mlp_kernel, turn),
        out_shape=(
            jax.ShapeDtypeStruct((rows // 2, model), jnp.float32),
            jax.ShapeDtypeStruct((3, 2 * rows, width), jnp.float32),
        ),
        in_specs=smem(2) + whole(9) + anywhere(len(before)),
        out_specs=tuple(anywhere(2)),
        scratch_shapes=[
            pltpu.VMEM((rows, model), jnp.bfloat16),
            pltpu.VMEM((rows, model), jnp.float32),
            pltpu.VMEM((3, rows, width), jnp.float32),
            pltpu.SemaphoreType.DMA((4,)),
        ],
        input_output_aliases={11 + i: i for i in range(len(before))},
        compiler_params=params(8),
        cost_estimate=cost(6e9, 0),
        name="mlp",
    )(ids, block_order, *pieces, hidden, w_co, *weights, *before)


def over_head(x, size):
    return [x] + [lax.ppermute(x, "head", xor(size, j)) for j in range(1, size)]


def over_chips(x, size):
    return [x] + [lax.ppermute(x, "blk", xor(size, s)) for s in range(2, size, 2)]


def on_device(
    tokens, block_order, request_lengths, enc_lengths, w_qkv, w_out, enc_kv, w_cq, w_co, w_up,
    w_down, w_next,
):
    group = lax.axis_size("head")
    cycle = lax.axis_size("blk")
    width = w_qkv.shape[2]
    ids = jnp.stack([lax.axis_index("blk"), lax.axis_index("head")]).astype(jnp.int32)
    paired = cycle == 8

    rows = over_head(tokens, group)
    if paired:
        enc = over_chips(enc_kv, cycle)
    x, queries, kv, part = project(ids, rows, w_qkv, w_out)
    w_cq, w_co, w_up, w_down, w_next = fetch(
        ids, (w_cq, w_co, w_up, w_down, w_next), {0: width}, 34, (queries,)
    )
    if paired:
        kvs, parts = over_chips(kv, cycle), over_head(part, group)
        own = bundle([kvs, enc, parts], (w_up,))
        other = [lax.ppermute(y, "blk", xor(cycle, 1)) for y in own]
        kvs, enc, parts = zip(own, other)
        near = tuple(range(0, cycle, 2))
        sources = [(True, near), (True, tuple(s + 1 for s in near))]
    else:
        kvs, enc = [lax.all_gather(y, "blk", axis=0)[None] for y in (kv, enc_kv)]
        kvs, enc = list(kvs), list(enc)
        sources = [(False, tuple(range(cycle)))]
        halves = w_out.reshape(2, width // 2, -1)
        parts = [
            bundle([over_head(lax.dynamic_index_in_dim(halves, ids[0] % 2 ^ i, 0, False), group)], ())[0]
            for i in range(2)
        ]
    keys, values, cache = order(ids, block_order, kvs, sources)
    enc_keys, enc_values, w_out = prepare(ids, enc, sources, parts)
    w_out = w_out.reshape(group, width, -1)

    outs = ()
    for turn in range(2):
        attended = self_attention(turn, ids, block_order, request_lengths, queries, keys, values)
        hidden, crossed = cross_attention(
            turn, ids, block_order, request_lengths, enc_lengths, over_head(attended, group), x,
            w_out, w_cq, enc_keys, enc_values,
        )
        outs = mlp(
            turn, ids, block_order, over_head(crossed, group), hidden, w_co,
            (w_up, w_down, w_next), outs,
        )
    return (outs[0], cache, outs[1])


def solution(mesh):
    in_specs = (
        P(("blk", "head"), None),
        P(),
        P(),
        P(),
        P(None, None, "head"),
        P("head", None),
        P(None, "blk", "head"),
        P(),
        P(),
        P(),
        P(),
        P(None, None, "head"),
    )
    out_specs = (P(("blk", "head"), None), P(None, "blk", "head"), P(None, "blk", "head"))
    return jax.shard_map(
        on_device, mesh=mesh, in_specs=in_specs, out_specs=out_specs, check_vma=False
    )
```

```python
import functools
import math

import jax
import jax.numpy as jnp
from jax import lax
from jax.experimental import pallas as pl
from jax.experimental.pallas import tpu as pltpu
from jax.sharding import PartitionSpec as P

HEADS = 16
NEGATIVE = -1e30
SCALING = 0.125
EPSILON = 1e-05
TILE = 512
ALIGN = 256
ONES = 16
MIB = 1024 * 1024


def whole(count):
    return [pl.BlockSpec(memory_space=pltpu.VMEM)] * count


def anywhere(count):
    return [pl.BlockSpec(memory_space=pl.ANY)] * count


def smem(count):
    return [pl.BlockSpec(memory_space=pltpu.SMEM)] * count


def params(mib):
    return pltpu.CompilerParams(vmem_limit_bytes=mib * MIB)


def xor(size, bits):
    return [(i, i ^ bits) for i in range(size)]


def normalize(matrix):
    center = matrix - jnp.mean(matrix, axis=-1, keepdims=True)
    return center * lax.rsqrt(jnp.mean(center * center, axis=-1, keepdims=True) + EPSILON)


def cost(flops, moved):
    return pl.CostEstimate(flops=int(flops) // 20, bytes_accessed=int(moved) // 20, transcendentals=0)


def skipping(kernel, at, count):
    def body(*refs):
        kernel(*refs[:at], *refs[at + count :])

    return body


def placed(kernel):
    def body(*refs):
        kernel((lax.axis_index("blk"), lax.axis_index("head")), *refs)

    return body


def rows_at(index, rows):
    return pl.ds(pl.multiple_of(index * rows, rows), rows)


def sums_of(lengths_ref):
    sums, total = [], jnp.int32(0)
    for j in range(lengths_ref.shape[0]):
        total = total + lengths_ref[j]
        sums.append(total)
    return sums


def project_kernel(ids, x0, x1, x2, x3, w_ref, part_in, x_ref, q_ref, kv_ref, part_ref):
    part_ref[...] = part_in[...]
    for i, piece in enumerate((x0, x1, x2, x3)):
        x_ref[rows_at(ids[1] ^ i, x0.shape[0]), :] = piece[...]
    x = x_ref[...]
    for c in range(2):
        kv_ref[c] = jnp.dot(x, w_ref[1 + c], preferred_element_type=jnp.float32).astype(
            jnp.bfloat16
        )
    q_ref[...] = jnp.dot(x, w_ref[0], preferred_element_type=jnp.float32).astype(jnp.bfloat16)


def project(pieces, w_qkv, part):
    rows, width, model = 4 * pieces[0].shape[0], w_qkv.shape[2], pieces[0].shape[1]
    return pl.pallas_call(
        placed(project_kernel),
        out_shape=(
            jax.ShapeDtypeStruct((rows, model), jnp.bfloat16),
            jax.ShapeDtypeStruct((rows, width), jnp.bfloat16),
            jax.ShapeDtypeStruct((2, rows, width), jnp.bfloat16),
            jax.ShapeDtypeStruct(part.shape, jnp.bfloat16),
        ),
        in_specs=whole(6),
        out_specs=tuple(whole(4)),
        compiler_params=params(4),
        cost_estimate=cost(2 * rows * model * 3 * width, 2 * 3 * model * width),
        name="project",
    )(*pieces, w_qkv, part)


def fetch_kernel(cuts, ids, *refs):
    count, sem = len(cuts), refs[-1]
    copies = []
    for i, cut in enumerate(cuts):
        source, target = refs[i], refs[count + i]
        if cut == "columns":
            width = target.shape[1]
            source = source.at[:, pl.ds(pl.multiple_of(ids[1] * width, width), width)]
        if cut == "rows":
            source = source.at[rows_at(ids[0] % 2, target.shape[0]), :]
        copy = pltpu.make_async_copy(source, target, sem)
        copy.start()
        copies.append(copy)
    for copy in copies:
        copy.wait()


def fetch(arrays, shapes, cuts, room, after=()):
    count = len(arrays)
    return pl.pallas_call(
        placed(skipping(functools.partial(fetch_kernel, cuts), 1 + count, len(after))),
        out_shape=tuple(jax.ShapeDtypeStruct(s, a.dtype) for s, a in zip(shapes, arrays)),
        in_specs=anywhere(count + len(after)),
        out_specs=tuple(whole(count)),
        scratch_shapes=[pltpu.SemaphoreType.DMA],
        compiler_params=params(room),
        cost_estimate=cost(0, 2 * sum(math.prod(s) for s in shapes)),
        name="fetch",
    )(*arrays, *after)


def bundle_kernel(groups, *refs):
    at = sum(groups)
    for i, count in enumerate(groups):
        for j in range(count):
            refs[at + i][j] = refs[sum(groups[:i]) + j][...]


def bundle(groups, after):
    counts = [len(g) for g in groups]
    total = sum(counts)
    return pl.pallas_call(
        skipping(functools.partial(bundle_kernel, counts), total, len(after)),
        out_shape=tuple(jax.ShapeDtypeStruct((len(g),) + g[0].shape, g[0].dtype) for g in groups),
        in_specs=whole(total) + anywhere(len(after)),
        out_specs=tuple(whole(len(groups))),
        compiler_params=params(2),
        cost_estimate=cost(0, 2 * 2 * sum(len(g) * math.prod(g[0].shape) for g in groups)),
        name="bundle",
    )(*[x for g in groups for x in g], *after)


def turned(v_ref, vt_ref):
    def step(tile, carry):
        at = rows_at(tile, ALIGN)
        for pair in range(vt_ref.shape[0]):
            vt_ref[pair, :128, at] = v_ref[at, pair * 128 : (pair + 1) * 128].T
            vt_ref[pair, 128:, at] = jnp.ones((ONES, ALIGN), jnp.bfloat16)
        return carry

    lax.fori_loop(0, v_ref.shape[0] // ALIGN, step, 0)


def order_kernel(sources, ids, order_ref, *refs):
    passed_in, k_ref, vt_ref, cache_ref, passed_ref, v_ref, sem = refs[-7:]
    passing = pltpu.make_async_copy(passed_in, passed_ref, sem)
    passing.start()
    for ref, (relative, numbers) in zip(refs, sources):
        rows = ref.shape[2] // 2
        for piece, number in enumerate(numbers):
            block = ids[0] ^ number if relative else jnp.int32(number)
            for half in range(2):
                at = rows_at(order_ref[2 * block + half], rows)
                here = slice(half * rows, (half + 1) * rows)
                k_ref[at, :] = ref[piece, 0, here, :]
                v_ref[at, :] = ref[piece, 1, here, :]
    turned(v_ref, vt_ref)
    at = rows_at(ids[0], cache_ref.shape[1])
    cache_ref[0] = k_ref[at, :]
    cache_ref[1] = v_ref[at, :]
    passing.wait()


def order(block_order, chunks, sources, passed):
    rows, width = chunks[0].shape[2:]
    total = rows * sum(c.shape[0] for c in chunks)
    return pl.pallas_call(
        placed(functools.partial(order_kernel, sources)),
        out_shape=(
            jax.ShapeDtypeStruct((total, width), jnp.bfloat16),
            jax.ShapeDtypeStruct((width // 128, 128 + ONES, total), jnp.bfloat16),
            jax.ShapeDtypeStruct((2, rows, width), jnp.bfloat16),
            jax.ShapeDtypeStruct(passed.shape, jnp.bfloat16),
        ),
        in_specs=smem(1) + whole(len(chunks)) + anywhere(1),
        out_specs=tuple(whole(4)),
        scratch_shapes=[pltpu.VMEM((total, width), jnp.bfloat16), pltpu.SemaphoreType.DMA],
        compiler_params=params(4 + total * width * 2 // MIB),
        cost_estimate=cost(0, 5 * 2 * total * width),
        name="order",
    )(block_order, *chunks, passed)


def prepare_kernel(sources, ids, *refs):
    k_ref, vt_ref, w_ref, v_ref = refs[-4:]
    for ref, (relative, numbers) in zip(refs, sources):
        rows = ref.shape[2]
        for piece, number in enumerate(numbers):
            at = rows_at(ids[0] ^ number if relative else jnp.int32(number), rows)
            k_ref[at, :] = ref[piece, 0]
            v_ref[at, :] = ref[piece, 1]
    turned(v_ref, vt_ref)
    parts = refs[len(sources) : -4]
    for i, part in enumerate(parts):
        for j in range(part.shape[0]):
            w_ref[ids[1] ^ j, ids[0] % 2 ^ i] = part[j]


def prepare(chunks, sources, parts):
    rows, width = chunks[0].shape[2:]
    total = rows * sum(c.shape[0] for c in chunks)
    group, depth, model = parts[0].shape
    return pl.pallas_call(
        placed(functools.partial(prepare_kernel, sources)),
        out_shape=(
            jax.ShapeDtypeStruct((total, width), jnp.bfloat16),
            jax.ShapeDtypeStruct((width // 128, 128 + ONES, total), jnp.bfloat16),
            jax.ShapeDtypeStruct((group, 2, depth, model), jnp.bfloat16),
        ),
        in_specs=whole(len(chunks) + len(parts)),
        out_specs=tuple(whole(3)),
        scratch_shapes=[pltpu.VMEM((total, width), jnp.bfloat16)],
        compiler_params=params(4),
        cost_estimate=cost(0, 5 * 2 * total * width),
        name="prepare",
    )(*chunks, *parts)


def flash(queries, k_ref, vt_ref, low, high, least, most):
    rows, width = queries.shape
    pairs = width // 128
    lane = lax.broadcasted_iota(jnp.int32, (rows, 128), 1) // 64
    masked = []
    for pair in range(pairs):
        part = queries[:, pair * 128 : (pair + 1) * 128]
        part = (part.astype(jnp.float32) * SCALING).astype(jnp.bfloat16)
        zero = jnp.zeros_like(part)
        masked.append(
            jnp.concatenate([jnp.where(lane == 0, part, zero), jnp.where(lane == 1, part, zero)], axis=0)
        )
    begin = least // ALIGN * ALIGN

    def step(tile, carry):
        due = begin + tile * TILE
        start = pl.multiple_of(jnp.minimum(due, k_ref.shape[0] - TILE), ALIGN)
        keys = start + lax.broadcasted_iota(jnp.int32, (TILE, 2 * rows), 0)
        bias = jnp.where((keys >= jnp.maximum(low, due)) & (keys < high), 0.0, NEGATIVE)
        after = []
        for pair in range(pairs):
            peak, total = carry[pair]
            scores = lax.dot_general(
                k_ref[pl.ds(start, TILE), pair * 128 : (pair + 1) * 128],
                masked[pair],
                (((1,), (1,)), ((), ())),
                preferred_element_type=jnp.float32,
            )
            scores = scores + bias
            top = jnp.maximum(peak, jnp.max(scores, axis=0, keepdims=True))
            weights = jnp.exp(scores - top).astype(jnp.bfloat16)
            total = total * jnp.exp(peak - top) + jnp.dot(
                vt_ref[pair, :, pl.ds(start, TILE)], weights, preferred_element_type=jnp.float32
            )
            after.append((top, total))
        return tuple(after)

    empty = (
        jnp.full((1, 2 * rows), NEGATIVE, jnp.float32),
        jnp.zeros((128 + ONES, 2 * rows), jnp.float32),
    )
    tiles = (most - begin + TILE - 1) // TILE
    carry = lax.fori_loop(0, tiles, step, (empty,) * pairs)
    outs = []
    for _, total in carry:
        result = total[:128] / total[128:129]
        outs += [result[:64, :rows], result[64:, rows:]]
    return jnp.concatenate(outs, axis=0).T


def twice(base, rows):
    lane = lax.broadcasted_iota(jnp.int32, (1, 2 * rows), 1)
    return base + jnp.where(lane >= rows, lane - rows, lane)


def half_of(turn, ids, order_ref):
    first = order_ref[2 * ids[0]]
    second = order_ref[2 * ids[0] + 1]
    return jnp.where(first < second, turn, 1 - turn)


def self_kernel(turn, ids, order_ref, lengths_ref, q_ref, k_ref, v_ref, out_ref):
    rows = out_ref.shape[0]
    half = half_of(turn, ids, order_ref)
    queries = q_ref[rows_at(half, rows), :]
    base = order_ref[2 * ids[0] + half] * rows
    places = twice(base, rows)
    low = jnp.zeros_like(places)
    least = jnp.int32(0)
    for end in sums_of(lengths_ref):
        low = jnp.where(places >= end, end, low)
        least = jnp.where(base >= end, end, least)
    result = flash(queries, k_ref, v_ref, low, places + 1, least, base + rows)
    out_ref[...] = result.astype(jnp.bfloat16)


def self_attention(turn, block_order, lengths, queries, keys, values, after=()):
    rows, width = queries.shape
    return pl.pallas_call(
        placed(skipping(functools.partial(self_kernel, turn), 6, len(after))),
        out_shape=jax.ShapeDtypeStruct((rows // 2, width), jnp.bfloat16),
        in_specs=smem(2) + whole(3) + anywhere(len(after)),
        out_specs=whole(1)[0],
        compiler_params=params(4),
        cost_estimate=cost(2e11, 0),
        name="self_attention",
    )(block_order, lengths, queries, keys, values, *after)


def cross_kernel(
    turn, ids, order_ref, lengths_ref, encs_ref,
    a0, a1, a2, a3, x_ref, wo_ref, wq_ref, k_ref, v_ref, hidden_ref, out_ref,
):
    rows, width = a0.shape
    member = ids[1]
    half = half_of(turn, ids, order_ref)
    mixed = x_ref[rows_at(half, rows), :].astype(jnp.float32)
    for i, piece in enumerate((a0, a1, a2, a3)):
        mixed = mixed + jnp.dot(
            piece[...], wo_ref[member ^ i], preferred_element_type=jnp.float32
        )
    hidden = normalize(mixed)
    hidden_ref[...] = hidden
    queries = jnp.dot(
        hidden.astype(jnp.bfloat16), wq_ref[...], preferred_element_type=jnp.float32
    ).astype(jnp.bfloat16)
    base = order_ref[2 * ids[0] + half] * rows
    places = twice(base, rows)
    ends, encs = sums_of(lengths_ref), sums_of(encs_ref)
    low = jnp.zeros_like(places)
    least = jnp.int32(0)
    for end, enc in zip(ends, encs):
        low = jnp.where(places >= end, enc, low)
        least = jnp.where(base >= end, enc, least)
    high = jnp.full_like(places, encs[-1])
    most = encs[-1]
    for end, enc in zip(reversed(ends), reversed(encs)):
        high = jnp.where(places < end, enc, high)
        most = jnp.where(base + rows - 1 < end, enc, most)
    result = flash(queries, k_ref, v_ref, low, high, least, most)
    out_ref[...] = result.astype(jnp.bfloat16)


def cross_attention(turn, block_order, lengths, encs, pieces, x, w_out, w_cq, keys, values):
    rows, width = pieces[0].shape
    model = x.shape[1]
    return pl.pallas_call(
        placed(functools.partial(cross_kernel, turn)),
        out_shape=(
            jax.ShapeDtypeStruct((rows, model), jnp.float32),
            jax.ShapeDtypeStruct((rows, width), jnp.bfloat16),
        ),
        in_specs=smem(3) + whole(9),
        out_specs=tuple(whole(2)),
        compiler_params=params(5),
        cost_estimate=cost(2e11, 0),
        name="cross_attention",
    )(block_order, lengths, encs, *pieces, x, w_out, w_cq, keys, values)


PART = 1024


def mlp_kernel(
    turn, ids, order_ref, c0, c1, c2, c3, hidden_ref, wco_ref, up_ref, down_ref, wn_ref, *refs
):
    out_ref, next_ref, bf_ref, sum_ref, held_ref, sems = refs[-6:]
    member = ids[1]
    half = half_of(turn, ids, order_ref)
    rows, width = c0.shape
    mixed = hidden_ref[...]
    for i, piece in enumerate((c0, c1, c2, c3)):
        mixed = mixed + jnp.dot(
            piece[...], wco_ref[rows_at(member ^ i, width), :], preferred_element_type=jnp.float32
        )
    second = normalize(mixed)
    bf_ref[...] = second.astype(jnp.bfloat16)
    sum_ref[...] = second
    for i in range(up_ref.shape[1] // PART):
        at = slice(i * PART, (i + 1) * PART)
        raised = jnp.dot(bf_ref[...], up_ref[:, at], preferred_element_type=jnp.float32)
        inner = (raised * (1.0 + lax.erf(raised * (0.5**0.5))) * 0.5).astype(jnp.bfloat16)
        sum_ref[...] += jnp.dot(inner, down_ref[at, :], preferred_element_type=jnp.float32)
    output = normalize(sum_ref[...])
    sum_ref[...] = output
    own = pltpu.make_async_copy(
        sum_ref.at[rows_at(member % 2, rows // 2), :], out_ref, sems.at[3]
    )

    @pl.when(member // 2 == half)
    def _():
        own.start()

    bf_ref[...] = output.astype(jnp.bfloat16)
    copies = []
    for c in range(3):
        held_ref[c] = jnp.dot(bf_ref[...], wn_ref[c], preferred_element_type=jnp.float32)
        copy = pltpu.make_async_copy(
            held_ref.at[c], next_ref.at[c, rows_at(half, rows), :], sems.at[c]
        )
        copy.start()
        copies.append(copy)
    for copy in copies:
        copy.wait()

    @pl.when(member // 2 == half)
    def _():
        own.wait()


def mlp(turn, block_order, pieces, hidden, w_co, weights, before):
    rows, width = pieces[0].shape
    model = w_co.shape[0]
    return pl.pallas_call(
        placed(functools.partial(mlp_kernel, turn)),
        out_shape=(
            jax.ShapeDtypeStruct((rows // 2, model), jnp.float32),
            jax.ShapeDtypeStruct((3, 2 * rows, width), jnp.float32),
        ),
        in_specs=smem(1) + whole(9) + anywhere(len(before)),
        out_specs=tuple(anywhere(2)),
        scratch_shapes=[
            pltpu.VMEM((rows, model), jnp.bfloat16),
            pltpu.VMEM((rows, model), jnp.float32),
            pltpu.VMEM((3, rows, width), jnp.float32),
            pltpu.SemaphoreType.DMA((4,)),
        ],
        input_output_aliases={10 + i: i for i in range(len(before))},
        compiler_params=params(8),
        cost_estimate=cost(6e9, 0),
        name="mlp",
    )(block_order, *pieces, hidden, w_co, *weights, *before)


def over_head(x, size):
    return [x] + [lax.ppermute(x, "head", xor(size, j)) for j in range(1, size)]


def over_chips(x, size):
    return [x] + [lax.ppermute(x, "blk", xor(size, s)) for s in range(2, size, 2)]


def on_device(
    tokens, block_order, request_lengths, enc_lengths, w_qkv, w_out, enc_kv, w_cq, w_co, w_up,
    w_down, w_next,
):
    group = lax.axis_size("head")
    cycle = lax.axis_size("blk")
    width = w_qkv.shape[2]
    paired = cycle == 8

    rows = over_head(tokens, group)
    tokens, w_qkv, part = fetch(
        (tokens, w_qkv, w_out),
        (tokens.shape, w_qkv.shape, (width // 2, w_out.shape[1])),
        ("", "", "rows"), 2,
    )
    x, queries, kv, part = project([tokens] + rows[1:], w_qkv, part)
    w_cq, w_co, w_up, w_down, w_next = fetch(
        (w_cq, w_co, w_up, w_down, w_next),
        ((w_cq.shape[0], width), w_co.shape, w_up.shape, w_down.shape, w_next.shape),
        ("columns", "", "", "", ""), 34, (queries,),
    )
    near = tuple(range(0, cycle, 2))
    if paired:
        kvs = over_chips(kv, cycle)
        parts = over_head(part, group)
        (kvs,) = bundle([kvs], [w_up] + parts[1:3])
        kvs = [kvs, lax.ppermute(kvs, "blk", xor(cycle, 1))]
        sources = [(True, near), (True, tuple(s + 1 for s in near))]
    else:
        kvs = [lax.all_gather(kv, "blk", axis=0)]
        sources = [(False, tuple(range(cycle)))]
    keys, values, cache, enc_kv = order(block_order, kvs, sources, enc_kv)
    attended = []
    for turn in range(2):
        mine = self_attention(
            turn, block_order, request_lengths, queries, keys, values, attended[0][:1] if turn else ()
        )
        attended.append(over_head(mine, group))
    if paired:
        own = bundle([parts, over_chips(enc_kv, cycle)], attended[1][:1] + attended[0][1:])
        parts, enc = zip(own, [lax.ppermute(y, "blk", xor(cycle, 1)) for y in own])
    else:
        enc = [lax.all_gather(enc_kv, "blk", axis=0)]
        halves = w_out.reshape(2, width // 2, -1)
        side = lax.axis_index("blk") % 2
        parts = [
            bundle([over_head(lax.dynamic_index_in_dim(halves, side ^ i, 0, False), group)], ())[0]
            for i in range(2)
        ]
    enc_keys, enc_values, w_out = prepare(enc, sources, parts)
    w_out = w_out.reshape(group, width, -1)

    outs = ()
    for turn in range(2):
        hidden, crossed = cross_attention(
            turn, block_order, request_lengths, enc_lengths, attended[turn], x, w_out,
            w_cq, enc_keys, enc_values,
        )
        outs = mlp(
            turn, block_order, over_head(crossed, group), hidden, w_co, (w_up, w_down, w_next),
            outs,
        )
    return (outs[0], cache, outs[1])


def solution(mesh):
    in_specs = (
        P(("blk", "head"), None),
        P(),
        P(),
        P(),
        P(None, None, "head"),
        P("head", None),
        P(None, "blk", "head"),
        P(),
        P(),
        P(),
        P(),
        P(None, None, "head"),
    )
    out_specs = (P(("blk", "head"), None), P(None, "blk", "head"), P(None, "blk", "head"))
    return jax.shard_map(
        on_device, mesh=mesh, in_specs=in_specs, out_specs=out_specs, check_vma=False
    )
```

```python
import functools
import math

import jax
import jax.numpy as jnp
from jax import lax
from jax.experimental import pallas as pl
from jax.experimental.pallas import tpu as pltpu
from jax.sharding import PartitionSpec as P

HEADS = 16
NEGATIVE = -1e30
SCALING = 0.125
EPSILON = 1e-05
TILE = 512
ALIGN = 256
ONES = 16
MIB = 1024 * 1024


def whole(count):
    return [pl.BlockSpec(memory_space=pltpu.VMEM)] * count


def anywhere(count):
    return [pl.BlockSpec(memory_space=pl.ANY)] * count


def smem(count):
    return [pl.BlockSpec(memory_space=pltpu.SMEM)] * count


def params(mib):
    return pltpu.CompilerParams(vmem_limit_bytes=mib * MIB)


def xor(size, bits):
    return [(i, i ^ bits) for i in range(size)]


def normalize(matrix):
    center = matrix - jnp.mean(matrix, axis=-1, keepdims=True)
    return center * lax.rsqrt(jnp.mean(center * center, axis=-1, keepdims=True) + EPSILON)


def cost(flops, moved):
    return pl.CostEstimate(flops=int(flops) // 20, bytes_accessed=int(moved) // 20, transcendentals=0)


def skipping(kernel, at, count):
    def body(*refs):
        kernel(*refs[:at], *refs[at + count :])

    return body


def placed(kernel):
    def body(*refs):
        kernel((lax.axis_index("blk"), lax.axis_index("head")), *refs)

    return body


def rows_at(index, rows):
    return pl.ds(pl.multiple_of(index * rows, rows), rows)


def sums_of(lengths_ref):
    sums, total = [], jnp.int32(0)
    for j in range(lengths_ref.shape[0]):
        total = total + lengths_ref[j]
        sums.append(total)
    return sums


def project_kernel(ids, x0, x1, x2, x3, w_ref, part_in, x_ref, q_ref, kv_ref, part_ref):
    part_ref[...] = part_in[...]
    for i, piece in enumerate((x0, x1, x2, x3)):
        x_ref[rows_at(ids[1] ^ i, x0.shape[0]), :] = piece[...]
    x = x_ref[...]
    for c in range(2):
        kv_ref[c] = jnp.dot(x, w_ref[1 + c], preferred_element_type=jnp.float32).astype(
            jnp.bfloat16
        )
    q_ref[...] = jnp.dot(x, w_ref[0], preferred_element_type=jnp.float32).astype(jnp.bfloat16)


def project(pieces, w_qkv, part):
    rows, width, model = 4 * pieces[0].shape[0], w_qkv.shape[2], pieces[0].shape[1]
    return pl.pallas_call(
        placed(project_kernel),
        out_shape=(
            jax.ShapeDtypeStruct((rows, model), jnp.bfloat16),
            jax.ShapeDtypeStruct((rows, width), jnp.bfloat16),
            jax.ShapeDtypeStruct((2, rows, width), jnp.bfloat16),
            jax.ShapeDtypeStruct(part.shape, jnp.bfloat16),
        ),
        in_specs=whole(6),
        out_specs=tuple(whole(4)),
        compiler_params=params(4),
        cost_estimate=cost(8e10, 0),
        name="project",
    )(*pieces, w_qkv, part)


def fetch_kernel(cuts, ids, *refs):
    count, sem = len(cuts), refs[-1]
    copies = []
    for i, cut in enumerate(cuts):
        source, target = refs[i], refs[count + i]
        if cut == "columns":
            width = target.shape[1]
            source = source.at[:, pl.ds(pl.multiple_of(ids[1] * width, width), width)]
        if cut == "rows":
            source = source.at[rows_at(ids[0] % 2, target.shape[0]), :]
        copy = pltpu.make_async_copy(source, target, sem)
        copy.start()
        copies.append(copy)
    for copy in copies:
        copy.wait()


def fetch(arrays, shapes, cuts, room, after=()):
    count = len(arrays)
    return pl.pallas_call(
        placed(skipping(functools.partial(fetch_kernel, cuts), 1 + count, len(after))),
        out_shape=tuple(jax.ShapeDtypeStruct(s, a.dtype) for s, a in zip(shapes, arrays)),
        in_specs=anywhere(count + len(after)),
        out_specs=tuple(whole(count)),
        scratch_shapes=[pltpu.SemaphoreType.DMA],
        compiler_params=params(room),
        cost_estimate=cost(0, 2 * sum(math.prod(s) for s in shapes)),
        name="fetch",
    )(*arrays, *after)


def bundle_kernel(groups, *refs):
    at = sum(groups)
    for i, count in enumerate(groups):
        for j in range(count):
            refs[at + i][j] = refs[sum(groups[:i]) + j][...]


def bundle(groups, after):
    counts = [len(g) for g in groups]
    total = sum(counts)
    return pl.pallas_call(
        skipping(functools.partial(bundle_kernel, counts), total, len(after)),
        out_shape=tuple(jax.ShapeDtypeStruct((len(g),) + g[0].shape, g[0].dtype) for g in groups),
        in_specs=whole(total) + anywhere(len(after)),
        out_specs=tuple(whole(len(groups))),
        compiler_params=params(2),
        cost_estimate=cost(0, 2 * 2 * sum(len(g) * math.prod(g[0].shape) for g in groups)),
        name="bundle",
    )(*[x for g in groups for x in g], *after)


def turned(v_ref, vt_ref):
    def step(tile, carry):
        at = rows_at(tile, ALIGN)
        for pair in range(vt_ref.shape[0]):
            vt_ref[pair, :128, at] = v_ref[at, pair * 128 : (pair + 1) * 128].T
            vt_ref[pair, 128:, at] = jnp.ones((ONES, ALIGN), jnp.bfloat16)
        return carry

    lax.fori_loop(0, v_ref.shape[0] // ALIGN, step, 0)


def order_kernel(sources, ids, order_ref, *refs):
    k_ref, vt_ref, cache_ref, v_ref = refs[-4:]
    for ref, (relative, numbers) in zip(refs, sources):
        rows = ref.shape[2] // 2
        for piece, number in enumerate(numbers):
            block = ids[0] ^ number if relative else jnp.int32(number)
            for half in range(2):
                at = rows_at(order_ref[2 * block + half], rows)
                here = slice(half * rows, (half + 1) * rows)
                k_ref[at, :] = ref[piece, 0, here, :]
                v_ref[at, :] = ref[piece, 1, here, :]
    turned(v_ref, vt_ref)
    at = rows_at(ids[0], cache_ref.shape[1])
    cache_ref[0] = k_ref[at, :]
    cache_ref[1] = v_ref[at, :]


def order(block_order, chunks, sources):
    rows, width = chunks[0].shape[2:]
    total = rows * sum(c.shape[0] for c in chunks)
    return pl.pallas_call(
        placed(functools.partial(order_kernel, sources)),
        out_shape=(
            jax.ShapeDtypeStruct((total, width), jnp.bfloat16),
            jax.ShapeDtypeStruct((width // 128, 128 + ONES, total), jnp.bfloat16),
            jax.ShapeDtypeStruct((2, rows, width), jnp.bfloat16),
        ),
        in_specs=smem(1) + whole(len(chunks)),
        out_specs=tuple(whole(3)),
        scratch_shapes=[pltpu.VMEM((total, width), jnp.bfloat16)],
        compiler_params=params(4 + total * width * 2 // MIB),
        cost_estimate=cost(0, 5 * 2 * total * width),
        name="order",
    )(block_order, *chunks)


def prepare_kernel(sources, ids, *refs):
    k_ref, vt_ref, w_ref, v_ref = refs[-4:]
    for ref, (relative, numbers) in zip(refs, sources):
        rows = ref.shape[2]
        for piece, number in enumerate(numbers):
            at = rows_at(ids[0] ^ number if relative else jnp.int32(number), rows)
            k_ref[at, :] = ref[piece, 0]
            v_ref[at, :] = ref[piece, 1]
    turned(v_ref, vt_ref)
    parts = refs[len(sources) : -4]
    for i, part in enumerate(parts):
        for j in range(part.shape[0]):
            w_ref[ids[1] ^ j, ids[0] % 2 ^ i] = part[j]


def prepare(chunks, sources, parts):
    rows, width = chunks[0].shape[2:]
    total = rows * sum(c.shape[0] for c in chunks)
    group, depth, model = parts[0].shape
    return pl.pallas_call(
        placed(functools.partial(prepare_kernel, sources)),
        out_shape=(
            jax.ShapeDtypeStruct((total, width), jnp.bfloat16),
            jax.ShapeDtypeStruct((width // 128, 128 + ONES, total), jnp.bfloat16),
            jax.ShapeDtypeStruct((group, 2, depth, model), jnp.bfloat16),
        ),
        in_specs=whole(len(chunks) + len(parts)),
        out_specs=tuple(whole(3)),
        scratch_shapes=[pltpu.VMEM((total, width), jnp.bfloat16)],
        compiler_params=params(4),
        cost_estimate=cost(0, 5 * 2 * total * width),
        name="prepare",
    )(*chunks, *parts)


def flash(queries, k_ref, vt_ref, low, high, least, most):
    rows, width = queries.shape
    pairs = width // 128
    lane = lax.broadcasted_iota(jnp.int32, (rows, 128), 1) // 64
    masked = []
    for pair in range(pairs):
        part = queries[:, pair * 128 : (pair + 1) * 128]
        part = (part.astype(jnp.float32) * SCALING).astype(jnp.bfloat16)
        zero = jnp.zeros_like(part)
        masked.append(
            jnp.concatenate([jnp.where(lane == 0, part, zero), jnp.where(lane == 1, part, zero)], axis=0)
        )
    begin = least // ALIGN * ALIGN

    def step(tile, carry):
        due = begin + tile * TILE
        start = pl.multiple_of(jnp.minimum(due, k_ref.shape[0] - TILE), ALIGN)
        keys = start + lax.broadcasted_iota(jnp.int32, (TILE, 2 * rows), 0)
        bias = jnp.where((keys >= jnp.maximum(low, due)) & (keys < high), 0.0, NEGATIVE)
        after = []
        for pair in range(pairs):
            peak, total = carry[pair]
            scores = lax.dot_general(
                k_ref[pl.ds(start, TILE), pair * 128 : (pair + 1) * 128],
                masked[pair],
                (((1,), (1,)), ((), ())),
                preferred_element_type=jnp.float32,
            )
            scores = scores + bias
            top = jnp.maximum(peak, jnp.max(scores, axis=0, keepdims=True))
            weights = jnp.exp(scores - top).astype(jnp.bfloat16)
            total = total * jnp.exp(peak - top) + jnp.dot(
                vt_ref[pair, :, pl.ds(start, TILE)], weights, preferred_element_type=jnp.float32
            )
            after.append((top, total))
        return tuple(after)

    empty = (
        jnp.full((1, 2 * rows), NEGATIVE, jnp.float32),
        jnp.zeros((128 + ONES, 2 * rows), jnp.float32),
    )
    tiles = (most - begin + TILE - 1) // TILE
    carry = lax.fori_loop(0, tiles, step, (empty,) * pairs)
    outs = []
    for _, total in carry:
        result = total[:128] / total[128:129]
        outs += [result[:64, :rows], result[64:, rows:]]
    return jnp.concatenate(outs, axis=0).T


def twice(base, rows):
    lane = lax.broadcasted_iota(jnp.int32, (1, 2 * rows), 1)
    return base + jnp.where(lane >= rows, lane - rows, lane)


def half_of(turn, ids, order_ref):
    first = order_ref[2 * ids[0]]
    second = order_ref[2 * ids[0] + 1]
    return jnp.where(first < second, turn, 1 - turn)


def self_kernel(turn, ids, order_ref, lengths_ref, q_ref, k_ref, v_ref, out_ref):
    rows = out_ref.shape[0]
    half = half_of(turn, ids, order_ref)
    queries = q_ref[rows_at(half, rows), :]
    base = order_ref[2 * ids[0] + half] * rows
    places = twice(base, rows)
    low = jnp.zeros_like(places)
    least = jnp.int32(0)
    for end in sums_of(lengths_ref):
        low = jnp.where(places >= end, end, low)
        least = jnp.where(base >= end, end, least)
    result = flash(queries, k_ref, v_ref, low, places + 1, least, base + rows)
    out_ref[...] = result.astype(jnp.bfloat16)


def self_attention(turn, block_order, lengths, queries, keys, values, after=()):
    rows, width = queries.shape
    return pl.pallas_call(
        placed(skipping(functools.partial(self_kernel, turn), 6, len(after))),
        out_shape=jax.ShapeDtypeStruct((rows // 2, width), jnp.bfloat16),
        in_specs=smem(2) + whole(3) + anywhere(len(after)),
        out_specs=whole(1)[0],
        compiler_params=params(4),
        cost_estimate=cost(2e11, 0),
        name="self_attention",
    )(block_order, lengths, queries, keys, values, *after)


def cross_kernel(
    turn, ids, order_ref, lengths_ref, encs_ref,
    a0, a1, a2, a3, x_ref, wo_ref, wq_ref, k_ref, v_ref, hidden_ref, out_ref,
):
    rows, width = a0.shape
    member = ids[1]
    half = half_of(turn, ids, order_ref)
    mixed = x_ref[rows_at(half, rows), :].astype(jnp.float32)
    for i, piece in enumerate((a0, a1, a2, a3)):
        mixed = mixed + jnp.dot(
            piece[...], wo_ref[member ^ i], preferred_element_type=jnp.float32
        )
    hidden = normalize(mixed)
    hidden_ref[...] = hidden
    queries = jnp.dot(
        hidden.astype(jnp.bfloat16), wq_ref[...], preferred_element_type=jnp.float32
    ).astype(jnp.bfloat16)
    base = order_ref[2 * ids[0] + half] * rows
    places = twice(base, rows)
    ends, encs = sums_of(lengths_ref), sums_of(encs_ref)
    low = jnp.zeros_like(places)
    least = jnp.int32(0)
    for end, enc in zip(ends, encs):
        low = jnp.where(places >= end, enc, low)
        least = jnp.where(base >= end, enc, least)
    high = jnp.full_like(places, encs[-1])
    most = encs[-1]
    for end, enc in zip(reversed(ends), reversed(encs)):
        high = jnp.where(places < end, enc, high)
        most = jnp.where(base + rows - 1 < end, enc, most)
    result = flash(queries, k_ref, v_ref, low, high, least, most)
    out_ref[...] = result.astype(jnp.bfloat16)


def cross_attention(turn, block_order, lengths, encs, pieces, x, w_out, w_cq, keys, values):
    rows, width = pieces[0].shape
    model = x.shape[1]
    return pl.pallas_call(
        placed(functools.partial(cross_kernel, turn)),
        out_shape=(
            jax.ShapeDtypeStruct((rows, model), jnp.float32),
            jax.ShapeDtypeStruct((rows, width), jnp.bfloat16),
        ),
        in_specs=smem(3) + whole(9),
        out_specs=tuple(whole(2)),
        compiler_params=params(5),
        cost_estimate=cost(2e11, 0),
        name="cross_attention",
    )(block_order, lengths, encs, *pieces, x, w_out, w_cq, keys, values)


PART = 1024


def mlp_kernel(
    turn, ids, order_ref, c0, c1, c2, c3, hidden_ref, wco_ref, up_ref, down_ref, wn_ref, *refs
):
    out_ref, next_ref, bf_ref, sum_ref, held_ref, sems = refs[-6:]
    member = ids[1]
    half = half_of(turn, ids, order_ref)
    rows, width = c0.shape
    mixed = hidden_ref[...]
    for i, piece in enumerate((c0, c1, c2, c3)):
        mixed = mixed + jnp.dot(
            piece[...], wco_ref[rows_at(member ^ i, width), :], preferred_element_type=jnp.float32
        )
    second = normalize(mixed)
    bf_ref[...] = second.astype(jnp.bfloat16)
    sum_ref[...] = second
    for i in range(up_ref.shape[1] // PART):
        at = slice(i * PART, (i + 1) * PART)
        raised = jnp.dot(bf_ref[...], up_ref[:, at], preferred_element_type=jnp.float32)
        inner = (raised * (1.0 + lax.erf(raised * (0.5**0.5))) * 0.5).astype(jnp.bfloat16)
        sum_ref[...] += jnp.dot(inner, down_ref[at, :], preferred_element_type=jnp.float32)
    output = normalize(sum_ref[...])
    sum_ref[...] = output
    own = pltpu.make_async_copy(
        sum_ref.at[rows_at(member % 2, rows // 2), :], out_ref, sems.at[3]
    )

    @pl.when(member // 2 == half)
    def _():
        own.start()

    bf_ref[...] = output.astype(jnp.bfloat16)
    copies = []
    for c in range(3):
        held_ref[c] = jnp.dot(bf_ref[...], wn_ref[c], preferred_element_type=jnp.float32)
        copy = pltpu.make_async_copy(
            held_ref.at[c], next_ref.at[c, rows_at(half, rows), :], sems.at[c]
        )
        copy.start()
        copies.append(copy)
    for copy in copies:
        copy.wait()

    @pl.when(member // 2 == half)
    def _():
        own.wait()


def mlp(turn, block_order, pieces, hidden, w_co, weights, before):
    rows, width = pieces[0].shape
    model = w_co.shape[0]
    return pl.pallas_call(
        placed(functools.partial(mlp_kernel, turn)),
        out_shape=(
            jax.ShapeDtypeStruct((rows // 2, model), jnp.float32),
            jax.ShapeDtypeStruct((3, 2 * rows, width), jnp.float32),
        ),
        in_specs=smem(1) + whole(9) + anywhere(len(before)),
        out_specs=tuple(anywhere(2)),
        scratch_shapes=[
            pltpu.VMEM((rows, model), jnp.bfloat16),
            pltpu.VMEM((rows, model), jnp.float32),
            pltpu.VMEM((3, rows, width), jnp.float32),
            pltpu.SemaphoreType.DMA((4,)),
        ],
        input_output_aliases={10 + i: i for i in range(len(before))},
        compiler_params=params(8),
        cost_estimate=cost(6e9, 0),
        name="mlp",
    )(block_order, *pieces, hidden, w_co, *weights, *before)


def over_head(x, size):
    return [x] + [lax.ppermute(x, "head", xor(size, j)) for j in range(1, size)]


def over_chips(x, size):
    return [x] + [lax.ppermute(x, "blk", xor(size, s)) for s in range(2, size, 2)]


def on_device(
    tokens, block_order, request_lengths, enc_lengths, w_qkv, w_out, enc_kv, w_cq, w_co, w_up,
    w_down, w_next,
):
    group = lax.axis_size("head")
    cycle = lax.axis_size("blk")
    width = w_qkv.shape[2]
    paired = cycle == 8

    rows = over_head(tokens, group)
    tokens, w_qkv, part = fetch(
        (tokens, w_qkv, w_out),
        (tokens.shape, w_qkv.shape, (width // 2, w_out.shape[1])),
        ("", "", "rows"), 2,
    )
    x, queries, kv, part = project([tokens] + rows[1:], w_qkv, part)
    enc = bundle([over_chips(enc_kv, cycle)], (queries,)) if paired else [queries]
    w_cq, w_co, w_up, w_down, w_next = fetch(
        (w_cq, w_co, w_up, w_down, w_next),
        ((w_cq.shape[0], width), w_co.shape, w_up.shape, w_down.shape, w_next.shape),
        ("columns", "", "", "", ""), 34, enc,
    )
    near = tuple(range(0, cycle, 2))
    if paired:
        kvs = over_chips(kv, cycle)
        parts = over_head(part, group)
        (kvs,) = bundle([kvs], [w_up] + parts[1:3])
        kvs = [kvs, lax.ppermute(kvs, "blk", xor(cycle, 1))]
        sources = [(True, near), (True, tuple(s + 1 for s in near))]
    else:
        kvs = [lax.all_gather(kv, "blk", axis=0)]
        sources = [(False, tuple(range(cycle)))]
    keys, values, cache = order(block_order, kvs, sources)
    attended = []
    for turn in range(2):
        mine = self_attention(
            turn, block_order, request_lengths, queries, keys, values, attended[0][:1] if turn else ()
        )
        attended.append(over_head(mine, group))
    if paired:
        own = bundle([parts], attended[1][:1] + attended[0][1:]) + enc
        parts, enc = zip(own, [lax.ppermute(y, "blk", xor(cycle, 1)) for y in own])
    else:
        enc = [lax.all_gather(enc_kv, "blk", axis=0)]
        halves = w_out.reshape(2, width // 2, -1)
        side = lax.axis_index("blk") % 2
        parts = [
            bundle([over_head(lax.dynamic_index_in_dim(halves, side ^ i, 0, False), group)], ())[0]
            for i in range(2)
        ]
    enc_keys, enc_values, w_out = prepare(enc, sources, parts)
    w_out = w_out.reshape(group, width, -1)

    outs = ()
    for turn in range(2):
        hidden, crossed = cross_attention(
            turn, block_order, request_lengths, enc_lengths, attended[turn], x, w_out,
            w_cq, enc_keys, enc_values,
        )
        outs = mlp(
            turn, block_order, over_head(crossed, group), hidden, w_co, (w_up, w_down, w_next),
            outs,
        )
    return (outs[0], cache, outs[1])


def solution(mesh):
    in_specs = (
        P(("blk", "head"), None),
        P(),
        P(),
        P(),
        P(None, None, "head"),
        P("head", None),
        P(None, "blk", "head"),
        P(),
        P(),
        P(),
        P(),
        P(None, None, "head"),
    )
    out_specs = (P(("blk", "head"), None), P(None, "blk", "head"), P(None, "blk", "head"))
    return jax.shard_map(
        on_device, mesh=mesh, in_specs=in_specs, out_specs=out_specs, check_vma=False
    )
```

```python
import functools
import math

import jax
import jax.numpy as jnp
from jax import lax
from jax.experimental import pallas as pl
from jax.experimental.pallas import tpu as pltpu
from jax.sharding import PartitionSpec as P

HEADS = 16
NEGATIVE = -1e30
SCALING = 0.125
EPSILON = 1e-05
TILE = 512
ALIGN = 256
ONES = 16
MIB = 1024 * 1024


def whole(count):
    return [pl.BlockSpec(memory_space=pltpu.VMEM)] * count


def anywhere(count):
    return [pl.BlockSpec(memory_space=pl.ANY)] * count


def smem(count):
    return [pl.BlockSpec(memory_space=pltpu.SMEM)] * count


def params(mib):
    return pltpu.CompilerParams(vmem_limit_bytes=mib * MIB)


def xor(size, bits):
    return [(i, i ^ bits) for i in range(size)]


def normalize(matrix):
    center = matrix - jnp.mean(matrix, axis=-1, keepdims=True)
    return center * lax.rsqrt(jnp.mean(center * center, axis=-1, keepdims=True) + EPSILON)


def cost(flops, moved):
    return pl.CostEstimate(flops=int(flops) // 20, bytes_accessed=int(moved) // 20, transcendentals=0)


def skipping(kernel, at, count):
    def body(*refs):
        kernel(*refs[:at], *refs[at + count :])

    return body


def placed(kernel):
    def body(*refs):
        kernel((lax.axis_index("blk"), lax.axis_index("head")), *refs)

    return body


def rows_at(index, rows):
    return pl.ds(pl.multiple_of(index * rows, rows), rows)


def sums_of(lengths_ref):
    sums, total = [], jnp.int32(0)
    for j in range(lengths_ref.shape[0]):
        total = total + lengths_ref[j]
        sums.append(total)
    return sums


def project_kernel(ids, x0, x1, x2, x3, w_ref, part_in, x_ref, q_ref, kv_ref, part_ref):
    part_ref[...] = part_in[...]
    for i, piece in enumerate((x0, x1, x2, x3)):
        x_ref[rows_at(ids[1] ^ i, x0.shape[0]), :] = piece[...]
    x = x_ref[...]
    for c in range(2):
        kv_ref[c] = jnp.dot(x, w_ref[1 + c], preferred_element_type=jnp.float32).astype(
            jnp.bfloat16
        )
    q_ref[...] = jnp.dot(x, w_ref[0], preferred_element_type=jnp.float32).astype(jnp.bfloat16)


def project(pieces, w_qkv, part):
    rows, width, model = 4 * pieces[0].shape[0], w_qkv.shape[2], pieces[0].shape[1]
    return pl.pallas_call(
        placed(project_kernel),
        out_shape=(
            jax.ShapeDtypeStruct((rows, model), jnp.bfloat16),
            jax.ShapeDtypeStruct((rows, width), jnp.bfloat16),
            jax.ShapeDtypeStruct((2, rows, width), jnp.bfloat16),
            jax.ShapeDtypeStruct(part.shape, jnp.bfloat16),
        ),
        in_specs=whole(6),
        out_specs=tuple(whole(4)),
        compiler_params=params(4),
        cost_estimate=cost(8e10, 0),
        name="project",
    )(*pieces, w_qkv, part)


def fetch_kernel(cuts, ids, *refs):
    count, sem = len(cuts), refs[-1]
    copies = []
    for i, cut in enumerate(cuts):
        source, target = refs[i], refs[count + i]
        if cut == "columns":
            width = target.shape[1]
            source = source.at[:, pl.ds(pl.multiple_of(ids[1] * width, width), width)]
        if cut == "rows":
            source = source.at[rows_at(ids[0] % 2, target.shape[0]), :]
        copy = pltpu.make_async_copy(source, target, sem)
        copy.start()
        copies.append(copy)
    for copy in copies:
        copy.wait()


def fetch(arrays, shapes, cuts, room, after=()):
    count = len(arrays)
    return pl.pallas_call(
        placed(skipping(functools.partial(fetch_kernel, cuts), 1 + count, len(after))),
        out_shape=tuple(jax.ShapeDtypeStruct(s, a.dtype) for s, a in zip(shapes, arrays)),
        in_specs=anywhere(count + len(after)),
        out_specs=tuple(whole(count)),
        scratch_shapes=[pltpu.SemaphoreType.DMA],
        compiler_params=params(room),
        cost_estimate=cost(0, 2 * sum(math.prod(s) for s in shapes)),
        name="fetch",
    )(*arrays, *after)


def bundle_kernel(groups, *refs):
    at = sum(groups)
    for i, count in enumerate(groups):
        for j in range(count):
            refs[at + i][j] = refs[sum(groups[:i]) + j][...]


def bundle(groups, after):
    counts = [len(g) for g in groups]
    total = sum(counts)
    return pl.pallas_call(
        skipping(functools.partial(bundle_kernel, counts), total, len(after)),
        out_shape=tuple(jax.ShapeDtypeStruct((len(g),) + g[0].shape, g[0].dtype) for g in groups),
        in_specs=whole(total) + anywhere(len(after)),
        out_specs=tuple(whole(len(groups))),
        compiler_params=params(2),
        cost_estimate=cost(0, 2 * 2 * sum(len(g) * math.prod(g[0].shape) for g in groups)),
        name="bundle",
    )(*[x for g in groups for x in g], *after)


def turned(v_ref, vt_ref):
    def step(tile, carry):
        at = rows_at(tile, ALIGN)
        for pair in range(vt_ref.shape[0]):
            vt_ref[pair, :128, at] = v_ref[at, pair * 128 : (pair + 1) * 128].T
            vt_ref[pair, 128:, at] = jnp.ones((ONES, ALIGN), jnp.bfloat16)
        return carry

    lax.fori_loop(0, v_ref.shape[0] // ALIGN, step, 0)


def order_kernel(sources, ids, order_ref, *refs):
    k_ref, vt_ref, cache_ref, v_ref = refs[-4:]
    for ref, (relative, numbers) in zip(refs, sources):
        rows = ref.shape[2] // 2
        for piece, number in enumerate(numbers):
            block = ids[0] ^ number if relative else jnp.int32(number)
            for half in range(2):
                at = rows_at(order_ref[2 * block + half], rows)
                here = slice(half * rows, (half + 1) * rows)
                k_ref[at, :] = ref[piece, 0, here, :]
                v_ref[at, :] = ref[piece, 1, here, :]
    turned(v_ref, vt_ref)
    at = rows_at(ids[0], cache_ref.shape[1])
    cache_ref[0] = k_ref[at, :]
    cache_ref[1] = v_ref[at, :]


def order(block_order, chunks, sources):
    rows, width = chunks[0].shape[2:]
    total = rows * sum(c.shape[0] for c in chunks)
    return pl.pallas_call(
        placed(functools.partial(order_kernel, sources)),
        out_shape=(
            jax.ShapeDtypeStruct((total, width), jnp.bfloat16),
            jax.ShapeDtypeStruct((width // 128, 128 + ONES, total), jnp.bfloat16),
            jax.ShapeDtypeStruct((2, rows, width), jnp.bfloat16),
        ),
        in_specs=smem(1) + whole(len(chunks)),
        out_specs=tuple(whole(3)),
        scratch_shapes=[pltpu.VMEM((total, width), jnp.bfloat16)],
        compiler_params=params(4 + total * width * 2 // MIB),
        cost_estimate=cost(0, 5 * 2 * total * width),
        name="order",
    )(block_order, *chunks)


def prepare_kernel(sources, ids, *refs):
    k_ref, vt_ref, w_ref, v_ref = refs[-4:]
    for ref, (relative, numbers) in zip(refs, sources):
        rows = ref.shape[2]
        for piece, number in enumerate(numbers):
            at = rows_at(ids[0] ^ number if relative else jnp.int32(number), rows)
            k_ref[at, :] = ref[piece, 0]
            v_ref[at, :] = ref[piece, 1]
    turned(v_ref, vt_ref)
    parts = refs[len(sources) : -4]
    for i, part in enumerate(parts):
        for j in range(part.shape[0]):
            w_ref[ids[1] ^ j, ids[0] % 2 ^ i] = part[j]


def prepare(chunks, sources, parts, after=()):
    rows, width = chunks[0].shape[2:]
    total = rows * sum(c.shape[0] for c in chunks)
    group, depth, model = parts[0].shape
    return pl.pallas_call(
        placed(
            skipping(
                functools.partial(prepare_kernel, sources), 1 + len(chunks) + len(parts), len(after)
            )
        ),
        out_shape=(
            jax.ShapeDtypeStruct((total, width), jnp.bfloat16),
            jax.ShapeDtypeStruct((width // 128, 128 + ONES, total), jnp.bfloat16),
            jax.ShapeDtypeStruct((group, 2, depth, model), jnp.bfloat16),
        ),
        in_specs=whole(len(chunks) + len(parts)) + anywhere(len(after)),
        out_specs=tuple(whole(3)),
        scratch_shapes=[pltpu.VMEM((total, width), jnp.bfloat16)],
        compiler_params=params(4),
        cost_estimate=cost(0, 5 * 2 * total * width),
        name="prepare",
    )(*chunks, *parts, *after)


def flash(queries, k_ref, vt_ref, low, high, least, most):
    rows, width = queries.shape
    pairs = width // 128
    lane = lax.broadcasted_iota(jnp.int32, (rows, 128), 1) // 64
    masked = []
    for pair in range(pairs):
        part = queries[:, pair * 128 : (pair + 1) * 128]
        part = (part.astype(jnp.float32) * SCALING).astype(jnp.bfloat16)
        zero = jnp.zeros_like(part)
        masked.append(
            jnp.concatenate([jnp.where(lane == 0, part, zero), jnp.where(lane == 1, part, zero)], axis=0)
        )
    begin = least // ALIGN * ALIGN

    def step(tile, carry):
        due = begin + tile * TILE
        start = pl.multiple_of(jnp.minimum(due, k_ref.shape[0] - TILE), ALIGN)
        keys = start + lax.broadcasted_iota(jnp.int32, (TILE, 2 * rows), 0)
        bias = jnp.where((keys >= jnp.maximum(low, due)) & (keys < high), 0.0, NEGATIVE)
        after = []
        for pair in range(pairs):
            peak, total = carry[pair]
            scores = lax.dot_general(
                k_ref[pl.ds(start, TILE), pair * 128 : (pair + 1) * 128],
                masked[pair],
                (((1,), (1,)), ((), ())),
                preferred_element_type=jnp.float32,
            )
            scores = scores + bias
            top = jnp.maximum(peak, jnp.max(scores, axis=0, keepdims=True))
            weights = jnp.exp(scores - top).astype(jnp.bfloat16)
            total = total * jnp.exp(peak - top) + jnp.dot(
                vt_ref[pair, :, pl.ds(start, TILE)], weights, preferred_element_type=jnp.float32
            )
            after.append((top, total))
        return tuple(after)

    empty = (
        jnp.full((1, 2 * rows), NEGATIVE, jnp.float32),
        jnp.zeros((128 + ONES, 2 * rows), jnp.float32),
    )
    tiles = (most - begin + TILE - 1) // TILE
    carry = lax.fori_loop(0, tiles, step, (empty,) * pairs)
    outs = []
    for _, total in carry:
        result = total[:128] / total[128:129]
        outs += [result[:64, :rows], result[64:, rows:]]
    return jnp.concatenate(outs, axis=0).T


def twice(base, rows):
    lane = lax.broadcasted_iota(jnp.int32, (1, 2 * rows), 1)
    return base + jnp.where(lane >= rows, lane - rows, lane)


def half_of(turn, ids, order_ref):
    first = order_ref[2 * ids[0]]
    second = order_ref[2 * ids[0] + 1]
    return jnp.where(first < second, turn, 1 - turn)


def self_kernel(turn, ids, order_ref, lengths_ref, q_ref, k_ref, v_ref, out_ref):
    rows = out_ref.shape[0]
    half = half_of(turn, ids, order_ref)
    queries = q_ref[rows_at(half, rows), :]
    base = order_ref[2 * ids[0] + half] * rows
    places = twice(base, rows)
    low = jnp.zeros_like(places)
    least = jnp.int32(0)
    for end in sums_of(lengths_ref):
        low = jnp.where(places >= end, end, low)
        least = jnp.where(base >= end, end, least)
    result = flash(queries, k_ref, v_ref, low, places + 1, least, base + rows)
    out_ref[...] = result.astype(jnp.bfloat16)


def self_attention(turn, block_order, lengths, queries, keys, values, after=()):
    rows, width = queries.shape
    return pl.pallas_call(
        placed(skipping(functools.partial(self_kernel, turn), 6, len(after))),
        out_shape=jax.ShapeDtypeStruct((rows // 2, width), jnp.bfloat16),
        in_specs=smem(2) + whole(3) + anywhere(len(after)),
        out_specs=whole(1)[0],
        compiler_params=params(4),
        cost_estimate=cost(2e11, 0),
        name="self_attention",
    )(block_order, lengths, queries, keys, values, *after)


def cross_kernel(
    turn, ids, order_ref, lengths_ref, encs_ref,
    a0, a1, a2, a3, x_ref, wo_ref, wq_ref, k_ref, v_ref, hidden_ref, out_ref,
):
    rows, width = a0.shape
    member = ids[1]
    half = half_of(turn, ids, order_ref)
    mixed = x_ref[rows_at(half, rows), :].astype(jnp.float32)
    for i, piece in enumerate((a0, a1, a2, a3)):
        mixed = mixed + jnp.dot(
            piece[...], wo_ref[member ^ i], preferred_element_type=jnp.float32
        )
    hidden = normalize(mixed)
    hidden_ref[...] = hidden
    queries = jnp.dot(
        hidden.astype(jnp.bfloat16), wq_ref[...], preferred_element_type=jnp.float32
    ).astype(jnp.bfloat16)
    base = order_ref[2 * ids[0] + half] * rows
    places = twice(base, rows)
    ends, encs = sums_of(lengths_ref), sums_of(encs_ref)
    low = jnp.zeros_like(places)
    least = jnp.int32(0)
    for end, enc in zip(ends, encs):
        low = jnp.where(places >= end, enc, low)
        least = jnp.where(base >= end, enc, least)
    high = jnp.full_like(places, encs[-1])
    most = encs[-1]
    for end, enc in zip(reversed(ends), reversed(encs)):
        high = jnp.where(places < end, enc, high)
        most = jnp.where(base + rows - 1 < end, enc, most)
    result = flash(queries, k_ref, v_ref, low, high, least, most)
    out_ref[...] = result.astype(jnp.bfloat16)


def cross_attention(turn, block_order, lengths, encs, pieces, x, w_out, w_cq, keys, values):
    rows, width = pieces[0].shape
    model = x.shape[1]
    return pl.pallas_call(
        placed(functools.partial(cross_kernel, turn)),
        out_shape=(
            jax.ShapeDtypeStruct((rows, model), jnp.float32),
            jax.ShapeDtypeStruct((rows, width), jnp.bfloat16),
        ),
        in_specs=smem(3) + whole(9),
        out_specs=tuple(whole(2)),
        compiler_params=params(5),
        cost_estimate=cost(2e11, 0),
        name="cross_attention",
    )(block_order, lengths, encs, *pieces, x, w_out, w_cq, keys, values)


PART = 1024


def mlp_kernel(
    turn, ids, order_ref, c0, c1, c2, c3, hidden_ref, wco_ref, up_ref, down_ref, wn_ref, *refs
):
    out_ref, next_ref, bf_ref, sum_ref, held_ref, sems = refs[-6:]
    member = ids[1]
    half = half_of(turn, ids, order_ref)
    rows, width = c0.shape
    mixed = hidden_ref[...]
    for i, piece in enumerate((c0, c1, c2, c3)):
        mixed = mixed + jnp.dot(
            piece[...], wco_ref[rows_at(member ^ i, width), :], preferred_element_type=jnp.float32
        )
    second = normalize(mixed)
    bf_ref[...] = second.astype(jnp.bfloat16)
    sum_ref[...] = second
    for i in range(up_ref.shape[1] // PART):
        at = slice(i * PART, (i + 1) * PART)
        raised = jnp.dot(bf_ref[...], up_ref[:, at], preferred_element_type=jnp.float32)
        inner = (raised * (1.0 + lax.erf(raised * (0.5**0.5))) * 0.5).astype(jnp.bfloat16)
        sum_ref[...] += jnp.dot(inner, down_ref[at, :], preferred_element_type=jnp.float32)
    output = normalize(sum_ref[...])
    sum_ref[...] = output
    own = pltpu.make_async_copy(
        sum_ref.at[rows_at(member % 2, rows // 2), :], out_ref, sems.at[3]
    )

    @pl.when(member // 2 == half)
    def _():
        own.start()

    bf_ref[...] = output.astype(jnp.bfloat16)
    copies = []
    for c in range(3):
        held_ref[c] = jnp.dot(bf_ref[...], wn_ref[c], preferred_element_type=jnp.float32)
        copy = pltpu.make_async_copy(
            held_ref.at[c], next_ref.at[c, rows_at(half, rows), :], sems.at[c]
        )
        copy.start()
        copies.append(copy)
    for copy in copies:
        copy.wait()

    @pl.when(member // 2 == half)
    def _():
        own.wait()


def mlp(turn, block_order, pieces, hidden, w_co, weights, before):
    rows, width = pieces[0].shape
    model = w_co.shape[0]
    return pl.pallas_call(
        placed(functools.partial(mlp_kernel, turn)),
        out_shape=(
            jax.ShapeDtypeStruct((rows // 2, model), jnp.float32),
            jax.ShapeDtypeStruct((3, 2 * rows, width), jnp.float32),
        ),
        in_specs=smem(1) + whole(9) + anywhere(len(before)),
        out_specs=tuple(anywhere(2)),
        scratch_shapes=[
            pltpu.VMEM((rows, model), jnp.bfloat16),
            pltpu.VMEM((rows, model), jnp.float32),
            pltpu.VMEM((3, rows, width), jnp.float32),
            pltpu.SemaphoreType.DMA((4,)),
        ],
        input_output_aliases={10 + i: i for i in range(len(before))},
        compiler_params=params(8),
        cost_estimate=cost(6e9, 0),
        name="mlp",
    )(block_order, *pieces, hidden, w_co, *weights, *before)


def over_head(x, size):
    return [x] + [lax.ppermute(x, "head", xor(size, j)) for j in range(1, size)]


def over_chips(x, size):
    return [x] + [lax.ppermute(x, "blk", xor(size, s)) for s in range(2, size, 2)]


def on_device(
    tokens, block_order, request_lengths, enc_lengths, w_qkv, w_out, enc_kv, w_cq, w_co, w_up,
    w_down, w_next,
):
    group = lax.axis_size("head")
    cycle = lax.axis_size("blk")
    width = w_qkv.shape[2]
    paired = cycle == 8

    rows = over_head(tokens, group)
    tokens, w_qkv, part = fetch(
        (tokens, w_qkv, w_out),
        (tokens.shape, w_qkv.shape, (width // 2, w_out.shape[1])),
        ("", "", "rows"), 2,
    )
    x, queries, kv, part = project([tokens] + rows[1:], w_qkv, part)
    enc = bundle([over_chips(enc_kv, cycle)], (queries,)) if paired else [queries]
    w_cq, w_co, w_up, w_down, w_next = fetch(
        (w_cq, w_co, w_up, w_down, w_next),
        ((w_cq.shape[0], width), w_co.shape, w_up.shape, w_down.shape, w_next.shape),
        ("columns", "", "", "", ""), 34, enc,
    )
    near = tuple(range(0, cycle, 2))
    if paired:
        kvs = over_chips(kv, cycle)
        parts = over_head(part, group)
        (kvs,) = bundle([kvs], [w_up] + parts[1:3])
        kvs = [kvs, lax.ppermute(kvs, "blk", xor(cycle, 1))]
        sources = [(True, near), (True, tuple(s + 1 for s in near))]
    else:
        kvs = [lax.all_gather(kv, "blk", axis=0)]
        sources = [(False, tuple(range(cycle)))]
    keys, values, cache = order(block_order, kvs, sources)
    attended = []
    for turn in range(2):
        mine = self_attention(
            turn, block_order, request_lengths, queries, keys, values, attended[0][:1] if turn else ()
        )
        attended.append(over_head(mine, group))
    if paired:
        own = bundle([parts], attended[0][:1]) + enc
        parts, enc = zip(own, [lax.ppermute(y, "blk", xor(cycle, 1)) for y in own])
    else:
        enc = [lax.all_gather(enc_kv, "blk", axis=0)]
        halves = w_out.reshape(2, width // 2, -1)
        side = lax.axis_index("blk") % 2
        parts = [
            bundle([over_head(lax.dynamic_index_in_dim(halves, side ^ i, 0, False), group)], ())[0]
            for i in range(2)
        ]
    enc_keys, enc_values, w_out = prepare(
        enc, sources, parts, attended[1][:1] + attended[0][1:]
    )
    w_out = w_out.reshape(group, width, -1)

    outs = ()
    for turn in range(2):
        hidden, crossed = cross_attention(
            turn, block_order, request_lengths, enc_lengths, attended[turn], x, w_out,
            w_cq, enc_keys, enc_values,
        )
        outs = mlp(
            turn, block_order, over_head(crossed, group), hidden, w_co, (w_up, w_down, w_next),
            outs,
        )
    return (outs[0], cache, outs[1])


def solution(mesh):
    in_specs = (
        P(("blk", "head"), None),
        P(),
        P(),
        P(),
        P(None, None, "head"),
        P("head", None),
        P(None, "blk", "head"),
        P(),
        P(),
        P(),
        P(),
        P(None, None, "head"),
    )
    out_specs = (P(("blk", "head"), None), P(None, "blk", "head"), P(None, "blk", "head"))
    return jax.shard_map(
        on_device, mesh=mesh, in_specs=in_specs, out_specs=out_specs, check_vma=False
    )
```

```python
import functools
import math

import jax
import jax.numpy as jnp
from jax import lax
from jax.experimental import pallas as pl
from jax.experimental.pallas import tpu as pltpu
from jax.sharding import PartitionSpec as P

HEADS = 16
NEGATIVE = -1e30
SCALING = 0.125
EPSILON = 1e-05
TILE = 512
ALIGN = 256
ONES = 16
MIB = 1024 * 1024


def whole(count):
    return [pl.BlockSpec(memory_space=pltpu.VMEM)] * count


def anywhere(count):
    return [pl.BlockSpec(memory_space=pl.ANY)] * count


def smem(count):
    return [pl.BlockSpec(memory_space=pltpu.SMEM)] * count


def params(mib):
    return pltpu.CompilerParams(vmem_limit_bytes=mib * MIB)


def xor(size, bits):
    return [(i, i ^ bits) for i in range(size)]


def normalize(matrix):
    center = matrix - jnp.mean(matrix, axis=-1, keepdims=True)
    return center * lax.rsqrt(jnp.mean(center * center, axis=-1, keepdims=True) + EPSILON)


def cost(flops, moved):
    return pl.CostEstimate(flops=int(flops) // 20, bytes_accessed=int(moved) // 20, transcendentals=0)


def skipping(kernel, at, count):
    def body(*refs):
        kernel(*refs[:at], *refs[at + count :])

    return body


def placed(kernel):
    def body(*refs):
        kernel((lax.axis_index("blk"), lax.axis_index("head")), *refs)

    return body


def rows_at(index, rows):
    return pl.ds(pl.multiple_of(index * rows, rows), rows)


def sums_of(lengths_ref):
    sums, total = [], jnp.int32(0)
    for j in range(lengths_ref.shape[0]):
        total = total + lengths_ref[j]
        sums.append(total)
    return sums


def project_kernel(ids, x0, x1, x2, x3, w_ref, part_in, x_ref, q_ref, kv_ref, part_ref):
    part_ref[...] = part_in[...]
    for i, piece in enumerate((x0, x1, x2, x3)):
        x_ref[rows_at(ids[1] ^ i, x0.shape[0]), :] = piece[...]
    x = x_ref[...]
    for c in range(2):
        kv_ref[c] = jnp.dot(x, w_ref[1 + c], preferred_element_type=jnp.float32).astype(
            jnp.bfloat16
        )
    q_ref[...] = jnp.dot(x, w_ref[0], preferred_element_type=jnp.float32).astype(jnp.bfloat16)


def project(pieces, w_qkv, part):
    rows, width, model = 4 * pieces[0].shape[0], w_qkv.shape[2], pieces[0].shape[1]
    return pl.pallas_call(
        placed(project_kernel),
        out_shape=(
            jax.ShapeDtypeStruct((rows, model), jnp.bfloat16),
            jax.ShapeDtypeStruct((rows, width), jnp.bfloat16),
            jax.ShapeDtypeStruct((2, rows, width), jnp.bfloat16),
            jax.ShapeDtypeStruct(part.shape, jnp.bfloat16),
        ),
        in_specs=whole(6),
        out_specs=tuple(whole(4)),
        compiler_params=params(4),
        cost_estimate=cost(8e10, 0),
        name="project",
    )(*pieces, w_qkv, part)


def fetch_kernel(cuts, ids, *refs):
    count, sem = len(cuts), refs[-1]
    copies = []
    for i, cut in enumerate(cuts):
        source, target = refs[i], refs[count + i]
        if cut == "columns":
            width = target.shape[1]
            source = source.at[:, pl.ds(pl.multiple_of(ids[1] * width, width), width)]
        if cut == "rows":
            source = source.at[rows_at(ids[0] % 2, target.shape[0]), :]
        copy = pltpu.make_async_copy(source, target, sem)
        copy.start()
        copies.append(copy)
    for copy in copies:
        copy.wait()


def fetch(arrays, shapes, cuts, room, after=()):
    count = len(arrays)
    return pl.pallas_call(
        placed(skipping(functools.partial(fetch_kernel, cuts), 1 + count, len(after))),
        out_shape=tuple(jax.ShapeDtypeStruct(s, a.dtype) for s, a in zip(shapes, arrays)),
        in_specs=anywhere(count + len(after)),
        out_specs=tuple(whole(count)),
        scratch_shapes=[pltpu.SemaphoreType.DMA],
        compiler_params=params(room),
        cost_estimate=cost(0, 2 * sum(math.prod(s) for s in shapes)),
        name="fetch",
    )(*arrays, *after)


def bundle_kernel(groups, *refs):
    at = sum(groups)
    for i, count in enumerate(groups):
        for j in range(count):
            refs[at + i][j] = refs[sum(groups[:i]) + j][...]


def bundle(groups, after):
    counts = [len(g) for g in groups]
    total = sum(counts)
    return pl.pallas_call(
        skipping(functools.partial(bundle_kernel, counts), total, len(after)),
        out_shape=tuple(jax.ShapeDtypeStruct((len(g),) + g[0].shape, g[0].dtype) for g in groups),
        in_specs=whole(total) + anywhere(len(after)),
        out_specs=tuple(whole(len(groups))),
        compiler_params=params(2),
        cost_estimate=cost(0, 2 * 2 * sum(len(g) * math.prod(g[0].shape) for g in groups)),
        name="bundle",
    )(*[x for g in groups for x in g], *after)


def turned(v_ref, vt_ref):
    def step(tile, carry):
        at = rows_at(tile, ALIGN)
        for pair in range(vt_ref.shape[0]):
            vt_ref[pair, :128, at] = v_ref[at, pair * 128 : (pair + 1) * 128].T
            vt_ref[pair, 128:, at] = jnp.ones((ONES, ALIGN), jnp.bfloat16)
        return carry

    lax.fori_loop(0, v_ref.shape[0] // ALIGN, step, 0)


def order_kernel(sources, ids, order_ref, *refs):
    k_ref, vt_ref, cache_ref, v_ref = refs[-4:]
    for ref, (relative, numbers) in zip(refs, sources):
        rows = ref.shape[2] // 2
        for piece, number in enumerate(numbers):
            block = ids[0] ^ number if relative else jnp.int32(number)
            for half in range(2):
                at = rows_at(order_ref[2 * block + half], rows)
                here = slice(half * rows, (half + 1) * rows)
                k_ref[at, :] = ref[piece, 0, here, :]
                v_ref[at, :] = ref[piece, 1, here, :]
    turned(v_ref, vt_ref)
    at = rows_at(ids[0], cache_ref.shape[1])
    cache_ref[0] = k_ref[at, :]
    cache_ref[1] = v_ref[at, :]


def order(block_order, chunks, sources):
    rows, width = chunks[0].shape[2:]
    total = rows * sum(c.shape[0] for c in chunks)
    return pl.pallas_call(
        placed(functools.partial(order_kernel, sources)),
        out_shape=(
            jax.ShapeDtypeStruct((total, width), jnp.bfloat16),
            jax.ShapeDtypeStruct((width // 128, 128 + ONES, total), jnp.bfloat16),
            jax.ShapeDtypeStruct((2, rows, width), jnp.bfloat16),
        ),
        in_specs=smem(1) + whole(len(chunks)),
        out_specs=tuple(whole(3)),
        scratch_shapes=[pltpu.VMEM((total, width), jnp.bfloat16)],
        compiler_params=params(4 + total * width * 2 // MIB),
        cost_estimate=cost(0, 5 * 2 * total * width),
        name="order",
    )(block_order, *chunks)


def prepare_kernel(sources, ids, *refs):
    k_ref, vt_ref, w_ref, v_ref = refs[-4:]
    for ref, (relative, numbers) in zip(refs, sources):
        rows = ref.shape[2]
        for piece, number in enumerate(numbers):
            at = rows_at(ids[0] ^ number if relative else jnp.int32(number), rows)
            k_ref[at, :] = ref[piece, 0]
            v_ref[at, :] = ref[piece, 1]
    turned(v_ref, vt_ref)
    parts = refs[len(sources) : -4]
    for i, part in enumerate(parts):
        for j in range(part.shape[0]):
            w_ref[ids[1] ^ j, ids[0] % 2 ^ i] = part[j]


def prepare(chunks, sources, parts, after=()):
    rows, width = chunks[0].shape[2:]
    total = rows * sum(c.shape[0] for c in chunks)
    group, depth, model = parts[0].shape
    return pl.pallas_call(
        placed(
            skipping(
                functools.partial(prepare_kernel, sources), 1 + len(chunks) + len(parts), len(after)
            )
        ),
        out_shape=(
            jax.ShapeDtypeStruct((total, width), jnp.bfloat16),
            jax.ShapeDtypeStruct((width // 128, 128 + ONES, total), jnp.bfloat16),
            jax.ShapeDtypeStruct((group, 2, depth, model), jnp.bfloat16),
        ),
        in_specs=whole(len(chunks) + len(parts)) + anywhere(len(after)),
        out_specs=tuple(whole(3)),
        scratch_shapes=[pltpu.VMEM((total, width), jnp.bfloat16)],
        compiler_params=params(4),
        cost_estimate=cost(0, 5 * 2 * total * width),
        name="prepare",
    )(*chunks, *parts, *after)


def flash(queries, k_ref, vt_ref, low, high, least, most):
    rows, width = queries.shape
    pairs = width // 128
    lane = lax.broadcasted_iota(jnp.int32, (rows, 128), 1) // 64
    masked = []
    for pair in range(pairs):
        part = queries[:, pair * 128 : (pair + 1) * 128]
        part = (part.astype(jnp.float32) * SCALING).astype(jnp.bfloat16)
        zero = jnp.zeros_like(part)
        masked.append(
            jnp.concatenate([jnp.where(lane == 0, part, zero), jnp.where(lane == 1, part, zero)], axis=0)
        )
    begin = least // ALIGN * ALIGN

    def step(tile, carry):
        due = begin + tile * TILE
        start = pl.multiple_of(jnp.minimum(due, k_ref.shape[0] - TILE), ALIGN)
        keys = start + lax.broadcasted_iota(jnp.int32, (TILE, 2 * rows), 0)
        bias = jnp.where((keys >= jnp.maximum(low, due)) & (keys < high), 0.0, NEGATIVE)
        after = []
        for pair in range(pairs):
            peak, total = carry[pair]
            scores = lax.dot_general(
                k_ref[pl.ds(start, TILE), pair * 128 : (pair + 1) * 128],
                masked[pair],
                (((1,), (1,)), ((), ())),
                preferred_element_type=jnp.float32,
            )
            scores = scores + bias
            top = jnp.maximum(peak, jnp.max(scores, axis=0, keepdims=True))
            weights = jnp.exp(scores - top).astype(jnp.bfloat16)
            total = total * jnp.exp(peak - top) + jnp.dot(
                vt_ref[pair, :, pl.ds(start, TILE)], weights, preferred_element_type=jnp.float32
            )
            after.append((top, total))
        return tuple(after)

    empty = (
        jnp.full((1, 2 * rows), NEGATIVE, jnp.float32),
        jnp.zeros((128 + ONES, 2 * rows), jnp.float32),
    )
    tiles = (most - begin + TILE - 1) // TILE
    carry = lax.fori_loop(0, tiles, step, (empty,) * pairs)
    outs = []
    for _, total in carry:
        result = total[:128] / total[128:129]
        outs += [result[:64, :rows], result[64:, rows:]]
    return jnp.concatenate(outs, axis=0).T


def twice(base, rows):
    lane = lax.broadcasted_iota(jnp.int32, (1, 2 * rows), 1)
    return base + jnp.where(lane >= rows, lane - rows, lane)


def half_of(turn, ids, order_ref):
    first = order_ref[2 * ids[0]]
    second = order_ref[2 * ids[0] + 1]
    return jnp.where(first < second, turn, 1 - turn)


def self_kernel(turn, ids, order_ref, lengths_ref, q_ref, k_ref, v_ref, out_ref):
    rows = out_ref.shape[0]
    half = half_of(turn, ids, order_ref)
    queries = q_ref[rows_at(half, rows), :]
    base = order_ref[2 * ids[0] + half] * rows
    places = twice(base, rows)
    low = jnp.zeros_like(places)
    least = jnp.int32(0)
    for end in sums_of(lengths_ref):
        low = jnp.where(places >= end, end, low)
        least = jnp.where(base >= end, end, least)
    result = flash(queries, k_ref, v_ref, low, places + 1, least, base + rows)
    out_ref[...] = result.astype(jnp.bfloat16)


def self_attention(turn, block_order, lengths, queries, keys, values, after=()):
    rows, width = queries.shape
    return pl.pallas_call(
        placed(skipping(functools.partial(self_kernel, turn), 6, len(after))),
        out_shape=jax.ShapeDtypeStruct((rows // 2, width), jnp.bfloat16),
        in_specs=smem(2) + whole(3) + anywhere(len(after)),
        out_specs=whole(1)[0],
        compiler_params=params(4),
        cost_estimate=cost(2e11, 0),
        name="self_attention",
    )(block_order, lengths, queries, keys, values, *after)


def cross_kernel(
    turn, ids, order_ref, lengths_ref, encs_ref,
    a0, a1, a2, a3, x_ref, wo_ref, wq_ref, k_ref, v_ref, hidden_ref, out_ref,
):
    rows, width = a0.shape
    member = ids[1]
    half = half_of(turn, ids, order_ref)
    mixed = x_ref[rows_at(half, rows), :].astype(jnp.float32)
    for i, piece in enumerate((a0, a1, a2, a3)):
        mixed = mixed + jnp.dot(
            piece[...], wo_ref[member ^ i], preferred_element_type=jnp.float32
        )
    hidden = normalize(mixed)
    hidden_ref[...] = hidden
    queries = jnp.dot(
        hidden.astype(jnp.bfloat16), wq_ref[...], preferred_element_type=jnp.float32
    ).astype(jnp.bfloat16)
    base = order_ref[2 * ids[0] + half] * rows
    places = twice(base, rows)
    ends, encs = sums_of(lengths_ref), sums_of(encs_ref)
    low = jnp.zeros_like(places)
    least = jnp.int32(0)
    for end, enc in zip(ends, encs):
        low = jnp.where(places >= end, enc, low)
        least = jnp.where(base >= end, enc, least)
    high = jnp.full_like(places, encs[-1])
    most = encs[-1]
    for end, enc in zip(reversed(ends), reversed(encs)):
        high = jnp.where(places < end, enc, high)
        most = jnp.where(base + rows - 1 < end, enc, most)
    result = flash(queries, k_ref, v_ref, low, high, least, most)
    out_ref[...] = result.astype(jnp.bfloat16)


def cross_attention(turn, block_order, lengths, encs, pieces, x, w_out, w_cq, keys, values):
    rows, width = pieces[0].shape
    model = x.shape[1]
    return pl.pallas_call(
        placed(functools.partial(cross_kernel, turn)),
        out_shape=(
            jax.ShapeDtypeStruct((rows, model), jnp.float32),
            jax.ShapeDtypeStruct((rows, width), jnp.bfloat16),
        ),
        in_specs=smem(3) + whole(9),
        out_specs=tuple(whole(2)),
        compiler_params=params(5),
        cost_estimate=cost(2e11, 0),
        name="cross_attention",
    )(block_order, lengths, encs, *pieces, x, w_out, w_cq, keys, values)


PART = 1024


def mlp_kernel(
    turn, ids, order_ref, c0, c1, c2, c3, hidden_ref, wco_ref, up_ref, down_ref, wn_ref, *refs
):
    out_ref, next_ref, bf_ref, sum_ref, held_ref, sems = refs[-6:]
    member = ids[1]
    half = half_of(turn, ids, order_ref)
    rows, width = c0.shape
    mixed = hidden_ref[...]
    for i, piece in enumerate((c0, c1, c2, c3)):
        mixed = mixed + jnp.dot(
            piece[...], wco_ref[rows_at(member ^ i, width), :], preferred_element_type=jnp.float32
        )
    second = normalize(mixed)
    bf_ref[...] = second.astype(jnp.bfloat16)
    sum_ref[...] = second
    for i in range(up_ref.shape[1] // PART):
        at = slice(i * PART, (i + 1) * PART)
        raised = jnp.dot(bf_ref[...], up_ref[:, at], preferred_element_type=jnp.float32)
        inner = (raised * (1.0 + lax.erf(raised * (0.5**0.5))) * 0.5).astype(jnp.bfloat16)
        sum_ref[...] += jnp.dot(inner, down_ref[at, :], preferred_element_type=jnp.float32)
    output = normalize(sum_ref[...])
    sum_ref[...] = output
    own = pltpu.make_async_copy(
        sum_ref.at[rows_at(member % 2, rows // 2), :], out_ref, sems.at[3]
    )

    @pl.when(member // 2 == half)
    def _():
        own.start()

    bf_ref[...] = output.astype(jnp.bfloat16)
    copies = []
    for c in range(3):
        held_ref[c] = jnp.dot(bf_ref[...], wn_ref[c], preferred_element_type=jnp.float32)
        copy = pltpu.make_async_copy(
            held_ref.at[c], next_ref.at[c, rows_at(half, rows), :], sems.at[c]
        )
        copy.start()
        copies.append(copy)
    for copy in copies:
        copy.wait()

    @pl.when(member // 2 == half)
    def _():
        own.wait()


def mlp(turn, block_order, pieces, hidden, w_co, weights, before):
    rows, width = pieces[0].shape
    model = w_co.shape[0]
    return pl.pallas_call(
        placed(functools.partial(mlp_kernel, turn)),
        out_shape=(
            jax.ShapeDtypeStruct((rows // 2, model), jnp.float32),
            jax.ShapeDtypeStruct((3, 2 * rows, width), jnp.float32),
        ),
        in_specs=smem(1) + whole(9) + anywhere(len(before)),
        out_specs=tuple(anywhere(2)),
        scratch_shapes=[
            pltpu.VMEM((rows, model), jnp.bfloat16),
            pltpu.VMEM((rows, model), jnp.float32),
            pltpu.VMEM((3, rows, width), jnp.float32),
            pltpu.SemaphoreType.DMA((4,)),
        ],
        input_output_aliases={10 + i: i for i in range(len(before))},
        compiler_params=params(8),
        cost_estimate=cost(6e9, 0),
        name="mlp",
    )(block_order, *pieces, hidden, w_co, *weights, *before)


def over_head(x, size):
    return [x] + [lax.ppermute(x, "head", xor(size, j)) for j in range(1, size)]


def over_chips(x, size):
    return [x] + [lax.ppermute(x, "blk", xor(size, s)) for s in range(2, size, 2)]


def on_device(
    tokens, block_order, request_lengths, enc_lengths, w_qkv, w_out, enc_kv, w_cq, w_co, w_up,
    w_down, w_next,
):
    group = lax.axis_size("head")
    cycle = lax.axis_size("blk")
    width = w_qkv.shape[2]
    paired = cycle == 8

    rows = over_head(tokens, group)
    tokens, w_qkv, part = fetch(
        (tokens, w_qkv, w_out),
        (tokens.shape, w_qkv.shape, (width // 2, w_out.shape[1])),
        ("", "", "rows"), 2,
    )
    x, queries, kv, part = project([tokens] + rows[1:], w_qkv, part)
    enc = bundle([over_chips(enc_kv, cycle)], (queries,)) if paired else [queries]
    w_cq, w_co, w_up, w_down, w_next = fetch(
        (w_cq, w_co, w_up, w_down, w_next),
        ((w_cq.shape[0], width), w_co.shape, w_up.shape, w_down.shape, w_next.shape),
        ("columns", "", "", "", ""), 34, enc,
    )
    near = tuple(range(0, cycle, 2))
    if paired:
        kvs = over_chips(kv, cycle)
        parts = [part] + [lax.ppermute(part, "head", xor(group, j)) for j in (1, 2)]
        parts.append(lax.ppermute(parts[2], "head", xor(group, 1)))
        (kvs,) = bundle([kvs], [w_up] + parts[1:3])
        kvs = [kvs, lax.ppermute(kvs, "blk", xor(cycle, 1))]
        sources = [(True, near), (True, tuple(s + 1 for s in near))]
    else:
        kvs = [lax.all_gather(kv, "blk", axis=0)]
        sources = [(False, tuple(range(cycle)))]
    keys, values, cache = order(block_order, kvs, sources)
    attended = []
    for turn in range(2):
        mine = self_attention(
            turn, block_order, request_lengths, queries, keys, values, attended[0][:1] if turn else ()
        )
        attended.append(over_head(mine, group))
    if paired:
        own = bundle([parts], attended[0][:1]) + enc
        parts, enc = zip(own, [lax.ppermute(y, "blk", xor(cycle, 1)) for y in own])
    else:
        enc = [lax.all_gather(enc_kv, "blk", axis=0)]
        halves = w_out.reshape(2, width // 2, -1)
        side = lax.axis_index("blk") % 2
        parts = [
            bundle([over_head(lax.dynamic_index_in_dim(halves, side ^ i, 0, False), group)], ())[0]
            for i in range(2)
        ]
    enc_keys, enc_values, w_out = prepare(
        enc, sources, parts, attended[1][:1] + attended[0][1:]
    )
    w_out = w_out.reshape(group, width, -1)

    outs = ()
    for turn in range(2):
        hidden, crossed = cross_attention(
            turn, block_order, request_lengths, enc_lengths, attended[turn], x, w_out,
            w_cq, enc_keys, enc_values,
        )
        outs = mlp(
            turn, block_order, over_head(crossed, group), hidden, w_co, (w_up, w_down, w_next),
            outs,
        )
    return (outs[0], cache, outs[1])


def solution(mesh):
    in_specs = (
        P(("blk", "head"), None),
        P(),
        P(),
        P(),
        P(None, None, "head"),
        P("head", None),
        P(None, "blk", "head"),
        P(),
        P(),
        P(),
        P(),
        P(None, None, "head"),
    )
    out_specs = (P(("blk", "head"), None), P(None, "blk", "head"), P(None, "blk", "head"))
    return jax.shard_map(
        on_device, mesh=mesh, in_specs=in_specs, out_specs=out_specs, check_vma=False
    )
```
